128 devices in a mesh: wide: 16 (over x, z), narrow: 8 (over y, core).
Axes of the slice: x: 4, y: 4, z: 4, core: 2. Of those that a mesh axis runs over, the one named last changes fastest.
Arguments:
- grad_kv: bfloat16 [8, 576, 7168], P(None, 'wide', 'narrow'), may hold values from -60 to 60
- grad_router: bfloat16 [8, 384, 7168], P(None, 'wide', 'narrow'), may hold values from -60 to 60
- momentum: float32 [48, 576, 7168], P('wide', None, 'narrow'), may hold values from -8 to 8
- owner: int32 [16], replicated, may hold values from 0 to 15, as said below
Outputs:
- update_kv: bfloat16 [8, 576, 7168], P(None, 'wide', 'narrow')
- update_router: bfloat16 [8, 384, 7168], P(None, 'wide', 'narrow')
- new_momentum: float32 [48, 576, 7168], P('wide', None, 'narrow')
The draws below stay inside these ranges and needn't reach their ends.
Inputs may be any that keep to these rules, and one draw needn't show every extreme that they name: Each owner index appears at most 3 times, and some index exactly 3 times.
All inputs are finite; a program needn't handle non-finite values.
Results may differ from the reference program's by a relative error of at most 0.015.
Values may be sent and summed in bfloat16 or wider, within the bound.
A program may use at most 192 MiB of HBM per device.

```python
import math
import jax
import jax.numpy as jnp
from jax import lax

D = 7168
KV_ROWS = 576
EXPERTS = 384
NS_ITERS = 3
LAYERS = 8
MATS = 16
MOST = 3
N_WIDE = 16
N_NARROW = 8


def scaled(key, noise):
    row_key, column_key = jax.random.split(key)
    shape = noise.shape
    row_scale = jnp.exp(jax.random.uniform(row_key, (shape[0], shape[1], 1), minval=-1.2, maxval=1.2))
    column_scale = jnp.exp(jax.random.uniform(column_key, (shape[0], 1, shape[2]), minval=-1.2, maxval=1.2))
    return jnp.clip(noise * row_scale * column_scale, -60.0, 60.0)


def draw_grad_kv(key, part):
    key = jax.random.fold_in(key, 11)
    noise_key, scale_key = jax.random.split(key, 2)
    shape = (LAYERS, KV_ROWS, D)
    noise = jnp.clip(jax.random.normal(noise_key, shape), -5.0, 5.0)
    return scaled(scale_key, noise).astype(jnp.bfloat16)


def draw_grad_router(key, part):
    key = jax.random.fold_in(key, 12)
    noise_key, scale_key = jax.random.split(key, 2)
    shape = (LAYERS, EXPERTS, D)
    noise = jnp.clip(jax.random.normal(noise_key, shape), -5.0, 5.0)
    return scaled(scale_key, noise).astype(jnp.bfloat16)


def draw_owner(key, part):
    key = jax.random.fold_in(key, 13)
    heavy_key, order_key, slot_key = jax.random.split(key, 3)
    heavy_owner = jax.random.randint(heavy_key, (), 0, N_WIDE).astype(jnp.int32)
    matrix_order = jax.random.permutation(order_key, MATS)
    spare_slots = jax.random.permutation(slot_key, (N_WIDE - 1) * MOST)[:MATS - MOST] // MOST
    others = (spare_slots + jnp.where(spare_slots >= heavy_owner, 1, 0)).astype(jnp.int32)
    ranked = jnp.concatenate([jnp.full((MOST,), heavy_owner, jnp.int32), others])
    return jnp.zeros((MATS,), jnp.int32).at[matrix_order].set(ranked)


def steps_of(rng, extent, cuts, low, largest):
    factor_of = 1.0
    for axis_at, shards_of in cuts:
        steps = jax.random.uniform(jax.random.fold_in(jax.random.fold_in(rng, 6), axis_at), (shards_of,), jnp.float32, low / len(cuts), largest / len(cuts))
        factor_of = factor_of * jnp.repeat(jnp.exp(steps), extent[axis_at] // shards_of).reshape((-1,) + (1,) * (len(extent) - 1 - axis_at))
    return factor_of


def normal_values(key, shape, width, reach, cuts=(), held_as=jnp.bfloat16):
    gain = steps_of(key, shape, cuts, -0.22, 0.18) if cuts else 1.0
    array = jax.random.normal(key, shape, jnp.float32) * width * gain
    return jnp.minimum(jnp.maximum(array, -reach), reach).astype(held_as)


def setup_inputs(seed: int = 0) -> dict:
    splits = jax.random.split(jax.random.key(seed), 5)
    return {
        "grad_kv": draw_grad_kv(jax.random.fold_in(splits[4], 71), 0),
        "grad_router": draw_grad_router(jax.random.fold_in(splits[4], 71), 0),
        "momentum": normal_values(splits[2], (N_WIDE * MOST, KV_ROWS, D), 1.5, 8.0, ((0, 16), (2, 8)), jnp.float32),
        "owner": draw_owner(jax.random.fold_in(splits[4], 71), 0),
    }


MOMENTUM_DECAY = 0.95
POLY_LINEAR = 3.4445
POLY_CUBIC = -4.775
POLY_QUINTIC = 2.0315
EPSILON = 1e-07
HALF_ROOT = 0.7071067811865476
FULL = lax.Precision.HIGHEST

def rotate(matrix):
    row_count = matrix.shape[0]
    block_width = D // N_NARROW
    blocks = matrix.reshape(row_count, N_NARROW, block_width)
    for bit_pos in range(N_NARROW.bit_length() - 1):
        stride = 1 << bit_pos
        paired = blocks.reshape(row_count, N_NARROW // (2 * stride), 2, stride, block_width).astype(jnp.float32)
        lower_half = paired[:, :, 0]
        upper_half = paired[:, :, 1]
        mixed = jnp.stack([lower_half + upper_half, lower_half - upper_half], axis=2) * HALF_ROOT
        blocks = mixed.astype(jnp.bfloat16).reshape(row_count, N_NARROW, block_width)
    return blocks.reshape(row_count, D)

def gram_matrix(iterate):
    return jnp.dot(iterate, iterate.T, precision=FULL, preferred_element_type=jnp.float32)

def orthogonalize(push):
    rounded = push.astype(jnp.bfloat16).astype(jnp.float32)
    first_gram = gram_matrix(rounded)
    inverse_norm = 1.0 / (jnp.sqrt(jnp.trace(first_gram)) + EPSILON)
    iterate = inverse_norm * rounded
    current = inverse_norm * inverse_norm * first_gram
    for turn_index in range(NS_ITERS):
        if turn_index > 0:
            current = gram_matrix(iterate)
        polynomial = POLY_CUBIC * current + POLY_QUINTIC * jnp.dot(current, current, precision=FULL, preferred_element_type=jnp.float32)
        product = jnp.dot(polynomial, iterate, precision=FULL, preferred_element_type=jnp.float32)
        iterate = POLY_LINEAR * iterate + product
    return iterate

def reference(grad_kv, grad_router, momentum, owner):
    matrix_ids = jnp.arange(MATS, dtype=jnp.int32)
    same_owner = owner[None, :] == owner[:, None]
    earlier = matrix_ids[None, :] < matrix_ids[:, None]
    slot_of = lax.optimization_barrier(jnp.sum(jnp.where(same_owner & earlier, 1, 0), axis=1)).astype(jnp.int32)
    home = (owner * MOST + slot_of).astype(jnp.int32)
    update_gain = 0.2 * math.sqrt(D)

    def advance(grad, home_slot, row_count):
        fresh = rotate(grad).astype(jnp.float32)
        state = lax.dynamic_index_in_dim(momentum, home_slot, 0, keepdims=False)[:row_count]
        new_state = MOMENTUM_DECAY * state + fresh
        push = fresh + MOMENTUM_DECAY * new_state
        update = (update_gain * orthogonalize(push)).astype(jnp.bfloat16)
        return (update, new_state)

    def kv_one(pair):
        return advance(pair[0], pair[1], KV_ROWS)

    def router_one(pair):
        return advance(pair[0], pair[1], EXPERTS)
    kv_update, kv_state = lax.map(kv_one, (grad_kv, home[0::2]))
    router_update, router_state = lax.map(router_one, (grad_router, home[1::2]))
    new_momentum = jnp.zeros((N_WIDE * MOST, KV_ROWS, D), jnp.float32)
    new_momentum = new_momentum.at[home[0::2]].set(kv_state)
    new_momentum = new_momentum.at[home[1::2], :EXPERTS].set(router_state)
    return (kv_update, router_update, new_momentum)
```

```python
import math

import jax
import jax.numpy as jnp
from jax import lax
from jax.experimental import pallas as pl
from jax.experimental.pallas import tpu as pltpu
from jax.sharding import PartitionSpec as P

D = 7168
KV = 576
EX = 384
LAYERS = 8
MATS = 16
MOST = 3
WIDE = 16
NARROW = 8
COLS = D // NARROW
KVL = KV // WIDE
EXL = EX // WIDE
BLK = 128
PADDED = 640

MOMENTUM_DECAY = 0.95
POLY_LINEAR = 3.4445
POLY_CUBIC = -4.775
POLY_QUINTIC = 2.0315
EPSILON = 1e-07
HALF_ROOT = 0.7071067811865476
GAIN = 0.2 * math.sqrt(D)

MESH = pl.DeviceIdType.MESH
F32 = jnp.float32
BF16 = jnp.bfloat16


def hops(offset):
    return sum(min(step, 4 - step) for step in offset)


WIDE_OFFSETS = sorted(
    [(i, j) for i in range(4) for j in range(4) if i or j], key=lambda o: -hops(o)
)
NARROW_OFFSETS = [(2, 0), (2, 1), (1, 0), (3, 0), (1, 1), (3, 1), (0, 1)]
UPPER = [(i, j) for i in range(5) for j in range(i, 5)]


def split(value):
    high = value.astype(BF16)
    low = (value - high.astype(F32)).astype(BF16)
    return high, low


def product(left, right):
    left_high, left_low = left
    right_high, right_low = right
    return jnp.dot(
        jnp.concatenate([left_high, left_high, left_low], axis=1),
        jnp.concatenate([right_high, right_low, right_high], axis=0),
        preferred_element_type=F32,
    )


def step_kernel(
    gkv,
    gr,
    mom_hbm,
    owner,
    out_kv,
    out_r,
    ma,
    momv,
    msend,
    marr,
    rk,
    rr,
    tk,
    tr,
    mk,
    mr,
    m36,
    ms,
    xk,
    xr,
    xak,
    xar,
    xmat,
    gb,
    ga,
    gh,
    gn,
    full,
    umat,
    uk,
    ur,
    slot_ref,
    load_sem,
    rot_send,
    rot_recv,
    back_send,
    back_recv,
    mom_send,
    mom_recv,
    x_send,
    x_recv,
    own_send,
    own_recv,
    own_local,
    red_send,
    red_recv,
    out_send,
    out_recv,
):
    w = lax.axis_index("wide")
    n = lax.axis_index("narrow")
    x, z = w // 4, w % 4
    y, c = n // 2, n % 2

    def wide_peer(offset, sign=1):
        return ((x + 4 + sign * offset[0]) % 4) * 4 + (z + 4 + sign * offset[1]) % 4

    def narrow_peer(offset, sign=1):
        return ((y + 4 + sign * offset[0]) % 4) * 2 + (c + offset[1]) % 2

    def remote(src, dst, send, recv, where):
        return pltpu.make_async_remote_copy(
            src_ref=src,
            dst_ref=dst,
            send_sem=send,
            recv_sem=recv,
            device_id=where,
            device_id_type=MESH,
        )

    loads = [
        pltpu.make_async_copy(mom_hbm.at[s], momv.at[s], load_sem.at[s]) for s in range(MOST)
    ]
    for load in loads:
        load.start()

    barrier = pltpu.get_barrier_semaphore()
    for offset in WIDE_OFFSETS:
        pl.semaphore_signal(
            barrier, inc=1, device_id={"wide": wide_peer(offset)}, device_id_type=MESH
        )
    for offset in NARROW_OFFSETS:
        pl.semaphore_signal(
            barrier, inc=1, device_id={"narrow": narrow_peer(offset)}, device_id_type=MESH
        )
    pl.semaphore_wait(barrier, len(WIDE_OFFSETS) + len(NARROW_OFFSETS))

    rot = []
    for i, offset in enumerate(NARROW_OFFSETS):
        to = narrow_peer(offset)
        for part, (src, dst) in enumerate(((gkv, rk), (gr, rr))):
            copy = remote(
                src.at[to],
                dst.at[n],
                rot_send.at[part, i],
                rot_recv.at[part, i],
                {"narrow": to},
            )
            copy.start()
            rot.append(copy)
    rk[n] = gkv[n]
    rr[n] = gr[n]

    owners = [owner[k] for k in range(MATS)]
    slots = []
    for k in range(MATS):
        taken = jnp.int32(0)
        for before in range(k):
            taken = taken + jnp.where(owners[before] == owners[k], 1, 0)
        slots.append(taken)
        slot_ref[k] = taken

    mom = []
    for s in range(MOST):
        odd = jnp.int32(0)
        for k in range(1, MATS, 2):
            odd = odd + jnp.where((owners[k] == w) & (slots[k] == s), 1, 0)
        loads[s].wait()
        is_router = jnp.full((KVL, COLS), odd, jnp.int32) == 1
        for j in range(WIDE):
            as_kv = momv[s, j * KVL : (j + 1) * KVL, :]
            as_router = momv[s, j * EXL : j * EXL + KVL, :]
            msend[s, j] = jnp.where(is_router, as_router, as_kv).astype(BF16)
        for i, offset in enumerate(WIDE_OFFSETS):
            to = wide_peer(offset)
            copy = remote(
                msend.at[s, to],
                marr.at[w, s],
                mom_send.at[s, i],
                mom_recv.at[s, i],
                {"wide": to},
            )
            copy.start()
            mom.append(copy)
        marr[w, s] = msend[s, w]

    def rotate(source, target):
        def column(t, carry):
            cols = pl.ds(pl.multiple_of(t * BLK, BLK), BLK)
            blocks = [source[b, :, cols].astype(F32) for b in range(NARROW)]
            for bit in range(3):
                stride = 1 << bit
                mixed = list(blocks)
                for b in range(NARROW):
                    if not b & stride:
                        low, high = blocks[b], blocks[b + stride]
                        mixed[b] = ((low + high) * HALF_ROOT).astype(BF16)
                        mixed[b + stride] = ((low - high) * HALF_ROOT).astype(BF16)
                        if bit < 2:
                            mixed[b] = mixed[b].astype(F32)
                            mixed[b + stride] = mixed[b + stride].astype(F32)
                blocks = mixed
            for b in range(NARROW):
                target[b, :, cols] = blocks[b]
            return carry

        lax.fori_loop(0, COLS // BLK, column, 0)

    back = []
    for part, (arrived, turned, final) in enumerate(((rk, tk, mk), (rr, tr, mr))):
        for i, offset in enumerate(NARROW_OFFSETS):
            rot[2 * i + part].wait_recv()
        rotate(arrived, turned)
        for i, offset in enumerate(NARROW_OFFSETS):
            to = narrow_peer(offset)
            copy = remote(
                turned.at[to],
                final.at[n],
                back_send.at[part, i],
                back_recv.at[part, i],
                {"narrow": to},
            )
            copy.start()
            back.append(copy)
        final[n] = turned[n]
    for copy in back:
        copy.wait_recv()
    for copy in mom:
        copy.wait_recv()

    def push(layer, carry):
        for part, (source, target, rows) in enumerate(((mk, xk, KVL), (mr, xr, EXL))):
            k = 2 * layer + part
            held = marr[owner[k], jnp.minimum(slot_ref[k], MOST - 1)][:rows].astype(F32)
            rounded = source[layer]
            fresh = rounded.astype(F32)
            state = MOMENTUM_DECAY * held + fresh
            target[layer] = (fresh + MOMENTUM_DECAY * state).astype(BF16)
            m36[k, 0:rows, :] = rounded
        return carry

    lax.fori_loop(0, LAYERS, push, 0)

    def x_copies(i, offset):
        to = wide_peer(offset)
        even = remote(
            xk.at[to // 2], xak.at[w], x_send.at[i], x_recv.at[i], {"wide": to}
        )
        odd = remote(xr.at[to // 2], xar.at[w], x_send.at[i], x_recv.at[i], {"wide": to})
        return to, even, odd

    is_even = w % 2 == 0
    for i, offset in enumerate(WIDE_OFFSETS):
        to, even, odd = x_copies(i, offset)

        @pl.when(to % 2 == 0)
        def _():
            even.start()

        @pl.when(to % 2 == 1)
        def _():
            odd.start()

    def stage(o, carry):
        for s in range(MOST):
            held = jnp.int32(0)
            for k in range(MATS):
                held = held + jnp.where((owner[k] == o) & (slot_ref[k] == s), k, 0)
            ms[s, o] = m36[held]
        return carry

    lax.fori_loop(0, WIDE, stage, 0)
    own = []
    for s in range(MOST):
        for i, offset in enumerate(WIDE_OFFSETS):
            to = wide_peer(offset)
            copy = remote(
                ms.at[s, to], ma.at[s, w], own_send.at[s, i], own_recv.at[s, i], {"wide": to}
            )
            copy.start()
            own.append(copy)
    stays = [pltpu.make_async_copy(ms.at[s, w], ma.at[s, w], own_local.at[s]) for s in range(MOST)]
    for copy in stays:
        copy.start()

    @pl.when(is_even)
    def _():
        xak[w] = xk[w // 2]
        for i, offset in enumerate(WIDE_OFFSETS):
            x_copies(i, offset)[1].wait_recv()
        for j in range(WIDE):
            xmat[j * KVL : (j + 1) * KVL, :] = xak[j].astype(F32)
        xmat[KV:, :] = jnp.zeros((PADDED - KV, COLS), F32)

    @pl.when(jnp.logical_not(is_even))
    def _():
        xar[w] = xr[w // 2]
        for i, offset in enumerate(WIDE_OFFSETS):
            x_copies(i, offset)[2].wait_recv()
        for j in range(WIDE):
            xmat[j * EXL : (j + 1) * EXL, :] = xar[j].astype(F32)
        xmat[EX:, :] = jnp.zeros((PADDED - EX, COLS), F32)

    values = xmat[...].astype(BF16)
    gram = lax.dot_general(
        values, values, (((1,), (1,)), ((), ())), preferred_element_type=F32
    )
    for b, (i, j) in enumerate(UPPER):
        gb[b] = gram[i * BLK : (i + 1) * BLK, j * BLK : (j + 1) * BLK]
    gb[15] = jnp.zeros((BLK, BLK), F32)

    partner = {"narrow": y * 2 + 1 - c}
    pair = remote(
        gb.at[pl.ds((1 - c) * 8, 8)], ga, red_send.at[0], red_recv.at[0], partner
    )
    pair.start()
    pair.wait_recv()
    gh[...] = gb[pl.ds(c * 8, 8)] + ga[...]
    scatter = []
    for i, step in enumerate((2, 1, 3)):
        to = (y + step) % 4
        copy = remote(
            gh.at[pl.ds(to * 2, 2)],
            gn.at[i],
            red_send.at[1 + i],
            red_recv.at[1 + i],
            {"narrow": to * 2 + c},
        )
        copy.start()
        scatter.append(copy)
    for copy in scatter:
        copy.wait_recv()
    mine = pl.ds(c * 8 + y * 2, 2)
    full[mine] = gh[pl.ds(y * 2, 2)] + gn[0] + gn[1] + gn[2]
    gather = []
    for i, step in enumerate((2, 1, 3)):
        to = (y + step) % 4
        copy = remote(
            full.at[mine],
            full.at[mine],
            red_send.at[4 + i],
            red_recv.at[4 + i],
            {"narrow": to * 2 + c},
        )
        copy.start()
        gather.append(copy)
    for copy in gather:
        copy.wait_recv()
    half = pl.ds(c * 8, 8)
    final_pair = remote(full.at[half], full.at[half], red_send.at[7], red_recv.at[7], partner)
    final_pair.start()
    final_pair.wait_recv()

    blocks = {}
    trace = jnp.zeros((1, 1), F32)
    eye = (
        lax.broadcasted_iota(jnp.int32, (BLK, BLK), 0)
        == lax.broadcasted_iota(jnp.int32, (BLK, BLK), 1)
    )
    for b, (i, j) in enumerate(UPPER):
        block = full[b]
        blocks[i, j] = block
        if i == j:
            trace = trace + jnp.sum(jnp.where(eye, block, 0.0), keepdims=True)
        else:
            blocks[j, i] = block.T
    first = jnp.concatenate(
        [jnp.concatenate([blocks[i, j] for j in range(5)], axis=1) for i in range(5)], axis=0
    )[:KV, :KV]
    inverse_norm = 1.0 / (jnp.sqrt(trace) + EPSILON)
    current = inverse_norm * inverse_norm * first

    diagonal = (
        lax.broadcasted_iota(jnp.int32, (KV, KV), 0)
        == lax.broadcasted_iota(jnp.int32, (KV, KV), 1)
    )

    def polynomial(gram_value, parts):
        return POLY_CUBIC * gram_value + POLY_QUINTIC * product(parts, parts)

    weight = None
    for turn in range(3):
        parts = split(current)
        cubic = split(polynomial(current, parts))
        if turn == 0:
            weight = jnp.where(diagonal, POLY_LINEAR, 0.0) + (
                cubic[0].astype(F32) + cubic[1].astype(F32)
            )
        else:
            weight = POLY_LINEAR * weight + product(cubic, split(weight))
        if turn < 2:
            half_way = POLY_LINEAR * current + product(cubic, parts)
            current = POLY_LINEAR * half_way + product(cubic, split(half_way))
    weight = split(weight * (inverse_norm * GAIN))
    weights = jnp.concatenate(weight, axis=1)
    values = values[:KV]
    umat[...] = jnp.dot(
        weights, jnp.concatenate([values, values], axis=0), preferred_element_type=F32
    )

    layer = w // 2

    def out_copies(i, offset):
        to = wide_peer(offset)
        where = {"wide": to}
        even = remote(uk.at[to], out_kv.at[layer], out_send.at[i], out_recv.at[i], where)
        odd = remote(ur.at[to], out_r.at[layer], out_send.at[i], out_recv.at[i], where)
        return even, odd

    @pl.when(is_even)
    def _():
        for j in range(WIDE):
            uk[j] = umat[j * KVL : (j + 1) * KVL, :].astype(BF16)
        for i, offset in enumerate(WIDE_OFFSETS):
            out_copies(i, offset)[0].start()
        out_kv[layer] = uk[w]

    @pl.when(jnp.logical_not(is_even))
    def _():
        for j in range(WIDE):
            ur[j] = umat[j * EXL : (j + 1) * EXL, :].astype(BF16)
        for i, offset in enumerate(WIDE_OFFSETS):
            out_copies(i, offset)[1].start()
        out_r[layer] = ur[w]

    for i, offset in enumerate(WIDE_OFFSETS):
        source = wide_peer(offset, -1)
        where = {"wide": wide_peer(offset)}
        even = remote(
            uk.at[0], out_kv.at[source // 2], out_send.at[i], out_recv.at[i], where
        )
        odd = remote(ur.at[0], out_r.at[source // 2], out_send.at[i], out_recv.at[i], where)

        @pl.when(source % 2 == 0)
        def _():
            even.wait_recv()

        @pl.when(source % 2 == 1)
        def _():
            odd.wait_recv()

    for copy in own:
        copy.wait_recv()
    for copy in stays:
        copy.wait()
    for copy in rot + back + mom + own + scatter + gather + [pair, final_pair]:
        copy.wait_send()
    for i, offset in enumerate(WIDE_OFFSETS):
        to, even, odd = x_copies(i, offset)

        @pl.when(to % 2 == 0)
        def _():
            even.wait_send()

        @pl.when(to % 2 == 1)
        def _():
            odd.wait_send()

    @pl.when(is_even)
    def _():
        for i, offset in enumerate(WIDE_OFFSETS):
            out_copies(i, offset)[0].wait_send()

    @pl.when(jnp.logical_not(is_even))
    def _():
        for i, offset in enumerate(WIDE_OFFSETS):
            out_copies(i, offset)[1].wait_send()


def state_kernel(owner, mom, ma, out):
    w = lax.axis_index("wide")
    s = pl.program_id(0)
    kind = jnp.int32(0)
    for k in range(MATS):
        slot = jnp.int32(0)
        for before in range(k):
            slot = slot + jnp.where(owner[before] == owner[k], 1, 0)
        kind = kind + jnp.where((owner[k] == w) & (slot == s), 1 + k % 2, 0)

    @pl.when(kind == 1)
    def _():
        for j in range(WIDE):
            rows = slice(j * KVL, (j + 1) * KVL)
            out[0, rows, :] = MOMENTUM_DECAY * mom[0, rows, :] + ma[0, j].astype(F32)

    @pl.when(kind == 2)
    def _():
        for j in range(WIDE):
            rows = slice(j * EXL, (j + 1) * EXL)
            out[0, rows, :] = MOMENTUM_DECAY * mom[0, rows, :] + ma[0, j, :EXL].astype(F32)
        out[0, EX:, :] = jnp.zeros((KV - EX, COLS), F32)

    @pl.when(kind == 0)
    def _():
        out[...] = jnp.zeros((1, KV, COLS), F32)


def local(grad_kv, grad_router, momentum, owner):
    vmem = pl.BlockSpec(memory_space=pltpu.VMEM)
    hbm = pl.BlockSpec(memory_space=pl.ANY)
    smem = pl.BlockSpec(memory_space=pltpu.SMEM)
    dma = pltpu.SemaphoreType.DMA
    kv_blocks = lambda count: pltpu.VMEM((count, KVL, COLS), BF16)
    r_blocks = lambda count: pltpu.VMEM((count, EXL, COLS), BF16)
    square = lambda count: pltpu.VMEM((count, BLK, BLK), F32)
    update_kv, update_router, arrived = pl.pallas_call(
        step_kernel,
        out_shape=(
            jax.ShapeDtypeStruct((LAYERS, KVL, COLS), BF16),
            jax.ShapeDtypeStruct((LAYERS, EXL, COLS), BF16),
            jax.ShapeDtypeStruct((MOST, WIDE, KVL, COLS), BF16),
        ),
        in_specs=[vmem, vmem, hbm, smem],
        out_specs=(vmem, vmem, hbm),
        scratch_shapes=[
            pltpu.VMEM((MOST, KV, COLS), F32),
            pltpu.VMEM((MOST, WIDE, KVL, COLS), BF16),
            pltpu.VMEM((WIDE, MOST, KVL, COLS), BF16),
            kv_blocks(NARROW),
            r_blocks(NARROW),
            kv_blocks(NARROW),
            r_blocks(NARROW),
            kv_blocks(LAYERS),
            r_blocks(LAYERS),
            kv_blocks(MATS),
            pltpu.VMEM((MOST, WIDE, KVL, COLS), BF16),
            kv_blocks(LAYERS),
            r_blocks(LAYERS),
            kv_blocks(WIDE),
            r_blocks(WIDE),
            pltpu.VMEM((PADDED, COLS), F32),
            square(16),
            square(8),
            square(8),
            pltpu.VMEM((3, 2, BLK, BLK), F32),
            square(16),
            pltpu.VMEM((KV, COLS), F32),
            kv_blocks(WIDE),
            r_blocks(WIDE),
            pltpu.SMEM((MATS,), jnp.int32),
            dma((MOST,)),
            dma((2, 7)),
            dma((2, 7)),
            dma((2, 7)),
            dma((2, 7)),
            dma((MOST, 15)),
            dma((MOST, 15)),
            dma((15,)),
            dma((15,)),
            dma((MOST, 15)),
            dma((MOST, 15)),
            dma((MOST,)),
            dma((8,)),
            dma((8,)),
            dma((15,)),
            dma((15,)),
        ],
        compiler_params=pltpu.CompilerParams(
            collective_id=0, has_side_effects=True, vmem_limit_bytes=60 * 2**20
        ),
        name="step",
    )(grad_kv, grad_router, momentum, owner)
    new_momentum = pl.pallas_call(
        state_kernel,
        grid=(MOST,),
        out_shape=jax.ShapeDtypeStruct((MOST, KV, COLS), F32),
        in_specs=[
            smem,
            pl.BlockSpec((1, KV, COLS), lambda s: (s, 0, 0)),
            pl.BlockSpec((1, WIDE, KVL, COLS), lambda s: (s, 0, 0, 0)),
        ],
        out_specs=pl.BlockSpec((1, KV, COLS), lambda s: (s, 0, 0)),
        compiler_params=pltpu.CompilerParams(vmem_limit_bytes=32 * 2**20),
        name="state",
    )(owner, momentum, arrived)
    return update_kv, update_router, new_momentum


def solution(mesh):
    in_specs = (
        P(None, "wide", "narrow"),
        P(None, "wide", "narrow"),
        P("wide", None, "narrow"),
        P(),
    )
    out_specs = (P(None, "wide", "narrow"), P(None, "wide", "narrow"), P("wide", None, "narrow"))
    return jax.shard_map(local, mesh=mesh, in_specs=in_specs, out_specs=out_specs, check_vma=False)
```

```python
import math

import jax
import jax.numpy as jnp
from jax import lax
from jax.experimental import pallas as pl
from jax.experimental.pallas import tpu as pltpu
from jax.sharding import PartitionSpec as P

D = 7168
KV = 576
EX = 384
LAYERS = 8
MATS = 16
MOST = 3
WIDE = 16
NARROW = 8
COLS = D // NARROW
KVL = KV // WIDE
EXL = EX // WIDE
BLK = 128
PADDED = 640
ROWS = 32
LANES = COLS + BLK
TILES = COLS // BLK
TAIL = KVL - ROWS

MOMENTUM_DECAY = 0.95
POLY_LINEAR = 3.4445
POLY_CUBIC = -4.775
POLY_QUINTIC = 2.0315
EPSILON = 1e-07
HALF_ROOT = 0.7071067811865476
GAIN = 0.2 * math.sqrt(D)

MESH = pl.DeviceIdType.MESH
F32 = jnp.float32
BF16 = jnp.bfloat16


def hops(offset):
    return sum(min(step, 4 - step) for step in offset)


WIDE_OFFSETS = sorted(
    [(i, j) for i in range(4) for j in range(4) if i or j], key=lambda o: -hops(o)
)
NARROW_OFFSETS = [(2, 0), (2, 1), (1, 0), (3, 0), (1, 1), (3, 1), (0, 1)]
UPPER = [(i, j) for i in range(5) for j in range(i, 5)]


def split(value):
    high = value.astype(BF16)
    low = (value - high.astype(F32)).astype(BF16)
    return high, low


def product(left, right):
    left_high, left_low = left
    right_high, right_low = right
    return jnp.dot(
        jnp.concatenate([left_high, left_high, left_low], axis=1),
        jnp.concatenate([right_high, right_low, right_high], axis=0),
        preferred_element_type=F32,
    )


def step_kernel(
    gkv,
    gr,
    mom_hbm,
    owner,
    out_kv,
    out_r,
    ma,
    momv,
    msend,
    marr,
    gp,
    rk,
    rr,
    tk,
    tr,
    mk,
    mr,
    mats,
    ms,
    xk,
    xr,
    xak,
    xar,
    xmat,
    xtail,
    tails,
    gb,
    ga,
    gh,
    gn,
    full,
    wmat,
    uk,
    ur,
    slot_ref,
    load_sem,
    rot_send,
    rot_recv,
    back_send,
    back_recv,
    mom_send,
    mom_recv,
    x_send,
    x_recv,
    own_send,
    own_recv,
    own_local,
    red_send,
    red_recv,
    out_send,
    out_recv,
):
    w = lax.axis_index("wide")
    n = lax.axis_index("narrow")
    x, z = w // 4, w % 4
    y, c = n // 2, n % 2
    is_even = w % 2 == 0
    is_odd = w % 2 == 1

    def wide_peer(offset):
        return ((x + offset[0]) % 4) * 4 + (z + offset[1]) % 4

    def narrow_peer(offset):
        return ((y + offset[0]) % 4) * 2 + (c + offset[1]) % 2

    def remote(src, dst, send, recv, where):
        return pltpu.make_async_remote_copy(
            src_ref=src,
            dst_ref=dst,
            send_sem=send,
            recv_sem=recv,
            device_id=where,
            device_id_type=MESH,
        )

    next_wide = {"wide": wide_peer((0, 1))}
    next_narrow = {"narrow": narrow_peer((0, 1))}

    def arrived(ref, sem, where):
        remote(ref, ref, sem, sem, where).wait_recv()

    def sent(ref, sem, where):
        remote(ref, ref, sem, sem, where).wait_send()

    loads = [
        pltpu.make_async_copy(mom_hbm.at[s], momv.at[s], load_sem.at[s]) for s in range(MOST)
    ]
    for load in loads:
        load.start()

    barrier = pltpu.get_barrier_semaphore()
    for offset in WIDE_OFFSETS:
        pl.semaphore_signal(
            barrier, inc=1, device_id={"wide": wide_peer(offset)}, device_id_type=MESH
        )
    for offset in NARROW_OFFSETS:
        pl.semaphore_signal(
            barrier, inc=1, device_id={"narrow": narrow_peer(offset)}, device_id_type=MESH
        )

    owners = [owner[k] for k in range(MATS)]
    slots = []
    for k in range(MATS):
        taken = jnp.int32(0)
        for before in range(k):
            taken = taken + jnp.where(owners[before] == owners[k], 1, 0)
        slots.append(taken)
        slot_ref[k] = taken

    tails[...] = jnp.zeros(tails.shape, F32)

    def pack_momentum(s):
        odd = jnp.int32(0)
        for k in range(1, MATS, 2):
            odd = odd + jnp.where((owners[k] == w) & (slots[k] == s), 1, 0)
        loads[s].wait()
        is_router = jnp.full((ROWS, COLS), odd, jnp.int32) == 1
        for j in range(WIDE):
            as_kv = momv[s, j * KVL : j * KVL + ROWS, :]
            as_router = momv[s, j * EXL : j * EXL + ROWS, :]
            msend[s, j, :, :COLS] = jnp.where(is_router, as_router, as_kv).astype(BF16)
            rest = momv[s, j * KVL + ROWS : (j + 1) * KVL, :]
            for t in range(TILES):
                tails[j, t * TAIL : (t + 1) * TAIL, :] = rest[:, t * BLK : (t + 1) * BLK]
        msend[s, :, :, COLS:] = tails[...].astype(BF16)

    def send_momentum(s):
        for offset in WIDE_OFFSETS:
            to = wide_peer(offset)
            remote(
                msend.at[s, to], marr.at[w, s], mom_send.at[0], mom_recv.at[0], {"wide": to}
            ).start()
        marr[w, s] = msend[s, w]

    pack_momentum(0)
    pl.semaphore_wait(barrier, len(WIDE_OFFSETS) + len(NARROW_OFFSETS))
    send_momentum(0)

    def gather_columns(part, source, target):
        for offset in NARROW_OFFSETS:
            to = narrow_peer(offset)
            remote(
                source.at[to], target.at[n], rot_send.at[part], rot_recv.at[part], {"narrow": to}
            ).start()
        target[n] = source[n]

    gather_columns(1, gr, rr)
    for t in range(TILES):
        cols = slice(t * BLK, (t + 1) * BLK)
        by_layer = jnp.swapaxes(gkv[:, :, cols].astype(F32), 0, 1)
        gp[:, :, cols] = by_layer[:, :ROWS].astype(BF16)
        tails[:LAYERS, t * TAIL : (t + 1) * TAIL, :] = by_layer[:, ROWS:]
    gp[:, :, COLS:] = tails[:LAYERS].astype(BF16)
    gather_columns(0, gp, rk)

    for s in range(1, MOST):
        pack_momentum(s)
        send_momentum(s)

    def rotate(source, target, count):
        def column(t, carry):
            cols = pl.ds(pl.multiple_of(t * BLK, BLK), BLK)
            blocks = [source[b, :, cols].astype(F32) for b in range(NARROW)]
            for bit in range(3):
                stride = 1 << bit
                mixed = list(blocks)
                for b in range(NARROW):
                    if not b & stride:
                        low, high = blocks[b], blocks[b + stride]
                        mixed[b] = ((low + high) * HALF_ROOT).astype(BF16)
                        mixed[b + stride] = ((low - high) * HALF_ROOT).astype(BF16)
                        if bit < 2:
                            mixed[b] = mixed[b].astype(F32)
                            mixed[b + stride] = mixed[b + stride].astype(F32)
                blocks = mixed
            for b in range(NARROW):
                target[b, :, cols] = blocks[b]
            return carry

        lax.fori_loop(0, count, column, 0)

    for part, source, turned, final in ((1, rr, tr, mr), (0, rk, tk, mk)):
        arrived(source.at[pl.ds(0, NARROW - 1)], rot_recv.at[part], next_narrow)
        rotate(source, turned, source.shape[2] // BLK)
        for offset in NARROW_OFFSETS:
            to = narrow_peer(offset)
            remote(
                turned.at[to], final.at[n], back_send.at[part], back_recv.at[part], {"narrow": to}
            ).start()
        final[n] = turned[n]
    for part, final in ((1, mr), (0, mk)):
        arrived(final.at[pl.ds(0, NARROW - 1)], back_recv.at[part], next_narrow)

    mats[...] = jnp.zeros(mats.shape, BF16)

    def by_matrix(layer, carry):
        mats[2 * layer] = mk[layer]
        mats[2 * layer + 1, :EXL, :COLS] = mr[layer]
        return carry

    lax.fori_loop(0, LAYERS, by_matrix, 0)

    def stage(o, carry):
        for s in range(MOST):
            held = jnp.int32(0)
            for k in range(MATS):
                held = held + jnp.where((owner[k] == o) & (slot_ref[k] == s), k, 0)
            ms[s, o] = mats[held]
        return carry

    lax.fori_loop(0, WIDE, stage, 0)
    arrived(marr.at[pl.ds(0, WIDE - 1)], mom_recv.at[0], next_wide)

    def push(layer, carry):
        for part, (source, target) in enumerate(((mk, xk), (mr, xr))):
            k = 2 * layer + part
            held = marr[owner[k], jnp.minimum(slot_ref[k], MOST - 1)]
            if part:
                held = held[:EXL, :COLS]
            fresh = source[layer].astype(F32)
            state = MOMENTUM_DECAY * held.astype(F32) + fresh
            target[layer] = (fresh + MOMENTUM_DECAY * state).astype(BF16)
        return carry

    lax.fori_loop(0, LAYERS, push, 0)

    for offset in WIDE_OFFSETS:
        to = wide_peer(offset)

        @pl.when(to % 2 == 0)
        def _():
            remote(
                xk.at[to // 2], xak.at[w], x_send.at[0], x_recv.at[0], {"wide": to}
            ).start()

        @pl.when(to % 2 == 1)
        def _():
            remote(
                xr.at[to // 2], xar.at[w], x_send.at[1], x_recv.at[0], {"wide": to}
            ).start()

    xmat[...] = jnp.zeros(xmat.shape, BF16)
    xtail[...] = jnp.zeros(xtail.shape, F32)

    @pl.when(is_even)
    def _():
        xak[w] = xk[w // 2]
        arrived(xak.at[pl.ds(0, WIDE - 1)], x_recv.at[0], next_wide)
        for j in range(WIDE):
            xmat[j * ROWS : (j + 1) * ROWS, :] = xak[j, :, :COLS]
            rest = xak[j, :, COLS:].astype(F32)
            for t in range(TILES):
                xtail[j * TAIL : (j + 1) * TAIL, t * BLK : (t + 1) * BLK] = rest[
                    t * TAIL : (t + 1) * TAIL
                ]
        xmat[WIDE * ROWS :, :] = xtail[...].astype(BF16)

    @pl.when(is_odd)
    def _():
        xar[w] = xr[w // 2]
        arrived(xar.at[pl.ds(0, WIDE - 1)], x_recv.at[0], next_wide)
        for j in range(WIDE):
            xmat[j * ROWS : j * ROWS + EXL, :] = xar[j]

    for s in range(MOST):
        for offset in WIDE_OFFSETS:
            to = wide_peer(offset)
            remote(
                ms.at[s, to], ma.at[s, w], own_send.at[0], own_recv.at[0], {"wide": to}
            ).start()
    stays = pltpu.make_async_copy(ms.at[:, w], ma.at[:, w], own_local.at[0])
    stays.start()

    gram = lax.dot_general(
        xmat[...], xmat[...], (((1,), (1,)), ((), ())), preferred_element_type=F32
    )
    for b, (i, j) in enumerate(UPPER):
        gb[b] = gram[i * BLK : (i + 1) * BLK, j * BLK : (j + 1) * BLK]
    gb[15] = jnp.zeros((BLK, BLK), F32)

    partner = {"narrow": y * 2 + 1 - c}
    pair = remote(
        gb.at[pl.ds((1 - c) * 8, 8)], ga, red_send.at[0], red_recv.at[0], partner
    )
    pair.start()
    pair.wait_recv()
    gh[...] = gb[pl.ds(c * 8, 8)] + ga[...]
    scatter = []
    for i, step in enumerate((2, 1, 3)):
        to = (y + step) % 4
        copy = remote(
            gh.at[pl.ds(to * 2, 2)],
            gn.at[i],
            red_send.at[1 + i],
            red_recv.at[1 + i],
            {"narrow": to * 2 + c},
        )
        copy.start()
        scatter.append(copy)
    for copy in scatter:
        copy.wait_recv()
    mine = pl.ds(c * 8 + y * 2, 2)
    full[mine] = gh[pl.ds(y * 2, 2)] + gn[0] + gn[1] + gn[2]
    gather = []
    for i, step in enumerate((2, 1, 3)):
        to = (y + step) % 4
        copy = remote(
            full.at[mine],
            full.at[mine],
            red_send.at[4 + i],
            red_recv.at[4 + i],
            {"narrow": to * 2 + c},
        )
        copy.start()
        gather.append(copy)
    for copy in gather:
        copy.wait_recv()
    half = pl.ds(c * 8, 8)
    final_pair = remote(full.at[half], full.at[half], red_send.at[7], red_recv.at[7], partner)
    final_pair.start()
    final_pair.wait_recv()

    blocks = {}
    trace = jnp.zeros((1, 1), F32)
    eye = (
        lax.broadcasted_iota(jnp.int32, (BLK, BLK), 0)
        == lax.broadcasted_iota(jnp.int32, (BLK, BLK), 1)
    )
    for b, (i, j) in enumerate(UPPER):
        block = full[b]
        blocks[i, j] = block
        if i == j:
            trace = trace + jnp.sum(jnp.where(eye, block, 0.0), keepdims=True)
        else:
            blocks[j, i] = block.T
    first = jnp.concatenate(
        [jnp.concatenate([blocks[i, j] for j in range(5)], axis=1) for i in range(5)], axis=0
    )[:KV, :KV]
    inverse_norm = 1.0 / (jnp.sqrt(trace) + EPSILON)
    current = inverse_norm * inverse_norm * first

    diagonal = (
        lax.broadcasted_iota(jnp.int32, (KV, KV), 0)
        == lax.broadcasted_iota(jnp.int32, (KV, KV), 1)
    )
    weight = None
    for turn in range(3):
        parts = split(current)
        cubic = split(POLY_CUBIC * current + POLY_QUINTIC * product(parts, parts))
        if turn == 0:
            weight = jnp.where(diagonal, POLY_LINEAR, 0.0) + (
                cubic[0].astype(F32) + cubic[1].astype(F32)
            )
        else:
            weight = POLY_LINEAR * weight + product(cubic, split(weight))
        if turn < 2:
            half_way = POLY_LINEAR * current + product(cubic, parts)
            current = POLY_LINEAR * half_way + product(cubic, split(half_way))
    wmat[...] = jnp.concatenate(split(weight * (inverse_norm * GAIN)), axis=1)

    layer = w // 2

    def apply(rows):
        values = xmat[:KV]
        return jnp.dot(
            wmat[rows, :], jnp.concatenate([values, values], axis=0), preferred_element_type=F32
        )

    @pl.when(is_even)
    def _():
        last = apply(pl.ds(WIDE * ROWS, WIDE * TAIL))
        for j in range(WIDE):
            for t in range(TILES):
                tails[j, t * TAIL : (t + 1) * TAIL, :] = last[
                    j * TAIL : (j + 1) * TAIL, t * BLK : (t + 1) * BLK
                ]
        uk[:, :, COLS:] = tails[...].astype(BF16)

    def outgoing(step, carry):
        group = (x + 2 + step) % 4
        chunk = apply(pl.ds(pl.multiple_of(group * BLK, BLK), BLK)).astype(BF16)
        for i in range(4):
            to = group * 4 + i
            rows = chunk[i * ROWS : (i + 1) * ROWS]

            @pl.when(is_even)
            def _():
                uk[to, :, :COLS] = rows

            @pl.when(is_odd)
            def _():
                ur[to] = rows[:EXL]

            @pl.when(jnp.logical_and(is_even, to != w))
            def _():
                remote(
                    uk.at[to], out_kv.at[layer], out_send.at[0], out_recv.at[0], {"wide": to}
                ).start()

            @pl.when(jnp.logical_and(is_odd, to != w))
            def _():
                remote(
                    ur.at[to], out_r.at[layer], out_send.at[0], out_recv.at[1], {"wide": to}
                ).start()

        return carry

    lax.fori_loop(0, 4, outgoing, 0)

    @pl.when(is_even)
    def _():
        out_kv[layer] = uk[w]
        arrived(out_kv.at[pl.ds(0, 7)], out_recv.at[0], next_wide)
        arrived(out_r.at[pl.ds(0, 8)], out_recv.at[1], next_wide)
        sent(uk.at[pl.ds(0, 15)], out_send.at[0], next_wide)
        sent(xk.at[pl.ds(0, 7)], x_send.at[0], next_wide)
        sent(xr.at[pl.ds(0, 8)], x_send.at[1], next_wide)

    @pl.when(is_odd)
    def _():
        out_r[layer] = ur[w]
        arrived(out_kv.at[pl.ds(0, 8)], out_recv.at[0], next_wide)
        arrived(out_r.at[pl.ds(0, 7)], out_recv.at[1], next_wide)
        sent(ur.at[pl.ds(0, 15)], out_send.at[0], next_wide)
        sent(xk.at[pl.ds(0, 8)], x_send.at[0], next_wide)
        sent(xr.at[pl.ds(0, 7)], x_send.at[1], next_wide)

    arrived(ma.at[:, pl.ds(0, WIDE - 1)], own_recv.at[0], next_wide)
    stays.wait()
    sent(ms.at[:, pl.ds(0, WIDE - 1)], own_send.at[0], next_wide)
    sent(msend.at[:, pl.ds(0, WIDE - 1)], mom_send.at[0], next_wide)
    for part, source, turned in ((0, gp, tk), (1, gr, tr)):
        sent(source.at[pl.ds(0, NARROW - 1)], rot_send.at[part], next_narrow)
        sent(turned.at[pl.ds(0, NARROW - 1)], back_send.at[part], next_narrow)
    for copy in scatter + gather + [pair, final_pair]:
        copy.wait_send()


def state_kernel(owner, mom, ma, out_kv, out_r, new, kv, router):
    w = lax.axis_index("wide")
    s = pl.program_id(0)
    kind = jnp.int32(0)
    for k in range(MATS):
        slot = jnp.int32(0)
        for before in range(k):
            slot = slot + jnp.where(owner[before] == owner[k], 1, 0)
        kind = kind + jnp.where((owner[k] == w) & (slot == s), 1 + k % 2, 0)

    @pl.when(kind == 1)
    def _():
        for j in range(WIDE):
            rows = slice(j * KVL, j * KVL + ROWS)
            new[0, rows, :] = MOMENTUM_DECAY * mom[0, rows, :] + ma[0, j, :, :COLS].astype(F32)
            rest = ma[0, j, :, COLS:].astype(F32)
            rows = slice(j * KVL + ROWS, (j + 1) * KVL)
            for t in range(TILES):
                cols = slice(t * BLK, (t + 1) * BLK)
                new[0, rows, cols] = (
                    MOMENTUM_DECAY * mom[0, rows, cols] + rest[t * TAIL : (t + 1) * TAIL]
                )

    @pl.when(kind == 2)
    def _():
        for j in range(WIDE):
            rows = slice(j * EXL, (j + 1) * EXL)
            new[0, rows, :] = MOMENTUM_DECAY * mom[0, rows, :] + ma[0, j, :EXL, :COLS].astype(F32)
        new[0, EX:, :] = jnp.zeros((KV - EX, COLS), F32)

    @pl.when(kind == 0)
    def _():
        new[...] = jnp.zeros((1, KV, COLS), F32)

    @pl.when(s == 0)
    def _():
        router[...] = out_r[...]
        for t in range(TILES):
            cols = slice(t * BLK, (t + 1) * BLK)
            kv[:ROWS, :, cols] = jnp.swapaxes(out_kv[:, :, cols].astype(F32), 0, 1).astype(BF16)
            rest = out_kv[:, :, COLS:].astype(F32)[:, t * TAIL : (t + 1) * TAIL]
            kv[ROWS:, :, cols] = jnp.swapaxes(rest, 0, 1).astype(BF16)


def local(grad_kv, grad_router, momentum, owner):
    vmem = pl.BlockSpec(memory_space=pltpu.VMEM)
    hbm = pl.BlockSpec(memory_space=pl.ANY)
    smem = pl.BlockSpec(memory_space=pltpu.SMEM)
    dma = pltpu.SemaphoreType.DMA
    kv_blocks = lambda *count: pltpu.VMEM(count + (ROWS, LANES), BF16)
    r_blocks = lambda count: pltpu.VMEM((count, EXL, COLS), BF16)
    square = lambda *count: pltpu.VMEM(count + (BLK, BLK), F32)
    update_kv, update_router, arrived = pl.pallas_call(
        step_kernel,
        out_shape=(
            jax.ShapeDtypeStruct((LAYERS, ROWS, LANES), BF16),
            jax.ShapeDtypeStruct((LAYERS, EXL, COLS), BF16),
            jax.ShapeDtypeStruct((MOST, WIDE, ROWS, LANES), BF16),
        ),
        in_specs=[vmem, vmem, hbm, smem],
        out_specs=(vmem, vmem, hbm),
        scratch_shapes=[
            pltpu.VMEM((MOST, KV, COLS), F32),
            kv_blocks(MOST, WIDE),
            kv_blocks(WIDE, MOST),
            kv_blocks(LAYERS),
            kv_blocks(NARROW),
            r_blocks(NARROW),
            kv_blocks(NARROW),
            r_blocks(NARROW),
            kv_blocks(LAYERS),
            r_blocks(LAYERS),
            kv_blocks(MATS),
            kv_blocks(MOST, WIDE),
            kv_blocks(LAYERS),
            r_blocks(LAYERS),
            kv_blocks(WIDE),
            r_blocks(WIDE),
            pltpu.VMEM((PADDED, COLS), BF16),
            pltpu.VMEM((PADDED - WIDE * ROWS, COLS), F32),
            pltpu.VMEM((WIDE, ROWS, BLK), F32),
            square(16),
            square(8),
            square(8),
            square(3, 2),
            square(16),
            pltpu.VMEM((KV, 2 * KV), BF16),
            kv_blocks(WIDE),
            r_blocks(WIDE),
            pltpu.SMEM((MATS,), jnp.int32),
            dma((MOST,)),
            dma((2,)),
            dma((2,)),
            dma((2,)),
            dma((2,)),
            dma((1,)),
            dma((1,)),
            dma((2,)),
            dma((1,)),
            dma((1,)),
            dma((1,)),
            dma((1,)),
            dma((8,)),
            dma((8,)),
            dma((1,)),
            dma((2,)),
        ],
        compiler_params=pltpu.CompilerParams(
            collective_id=0, has_side_effects=True, vmem_limit_bytes=60 * 2**20
        ),
        name="step",
    )(jnp.swapaxes(grad_kv, 0, 1), grad_router, momentum, owner)
    whole = lambda shape: pl.BlockSpec(shape, lambda s: (0,) * len(shape))
    new_momentum, kv, router = pl.pallas_call(
        state_kernel,
        grid=(MOST,),
        out_shape=(
            jax.ShapeDtypeStruct((MOST, KV, COLS), F32),
            jax.ShapeDtypeStruct((KVL, LAYERS, COLS), BF16),
            jax.ShapeDtypeStruct((LAYERS, EXL, COLS), BF16),
        ),
        in_specs=[
            smem,
            pl.BlockSpec((1, KV, COLS), lambda s: (s, 0, 0)),
            pl.BlockSpec((1, WIDE, ROWS, LANES), lambda s: (s, 0, 0, 0)),
            whole((LAYERS, ROWS, LANES)),
            whole((LAYERS, EXL, COLS)),
        ],
        out_specs=(
            pl.BlockSpec((1, KV, COLS), lambda s: (s, 0, 0)),
            whole((KVL, LAYERS, COLS)),
            whole((LAYERS, EXL, COLS)),
        ),
        compiler_params=pltpu.CompilerParams(vmem_limit_bytes=60 * 2**20),
        name="state",
    )(owner, momentum, arrived, update_kv, update_router)
    return jnp.swapaxes(kv, 0, 1), router, new_momentum


def solution(mesh):
    in_specs = (
        P(None, "wide", "narrow"),
        P(None, "wide", "narrow"),
        P("wide", None, "narrow"),
        P(),
    )
    out_specs = (P(None, "wide", "narrow"), P(None, "wide", "narrow"), P("wide", None, "narrow"))
    return jax.shard_map(local, mesh=mesh, in_specs=in_specs, out_specs=out_specs, check_vma=False)
```

```python
import math

import jax
import jax.numpy as jnp
from jax import lax
from jax.experimental import pallas as pl
from jax.experimental.pallas import tpu as pltpu
from jax.sharding import PartitionSpec as P

D = 7168
KV = 576
EX = 384
LAYERS = 8
MATS = 16
MOST = 3
WIDE = 16
NARROW = 8
COLS = D // NARROW
KVL = KV // WIDE
EXL = EX // WIDE
BLK = 128
PADDED = 640
ROWS = 32
LANES = COLS + BLK
TILES = COLS // BLK
TAIL = KVL - ROWS

MOMENTUM_DECAY = 0.95
POLY_LINEAR = 3.4445
POLY_CUBIC = -4.775
POLY_QUINTIC = 2.0315
EPSILON = 1e-07
HALF_ROOT = 0.7071067811865476
GAIN = 0.2 * math.sqrt(D)

MESH = pl.DeviceIdType.MESH
F32 = jnp.float32
BF16 = jnp.bfloat16


def hops(offset):
    return sum(min(step, 4 - step) for step in offset)


WIDE_OFFSETS = sorted(
    [(i, j) for i in range(4) for j in range(4) if i or j], key=lambda o: -hops(o)
)
NARROW_OFFSETS = [(2, 0), (2, 1), (1, 0), (3, 0), (1, 1), (3, 1), (0, 1)]
UPPER = [(i, j) for i in range(5) for j in range(i, 5)]


def split(value):
    high = value.astype(BF16)
    low = (value - high.astype(F32)).astype(BF16)
    return high, low


def product(left, right, terms=3):
    lefts = [left[0], left[0], left[1]][:terms]
    rights = [right[0], right[1], right[0]][:terms]
    return jnp.dot(
        jnp.concatenate(lefts, axis=1),
        jnp.concatenate(rights, axis=0),
        preferred_element_type=F32,
    )


def step_kernel(
    gkv,
    gr,
    mom_hbm,
    owner,
    out_kv,
    out_r,
    ma,
    momv,
    msend,
    marr,
    gp,
    rk,
    rr,
    tk,
    tr,
    mk,
    mr,
    mats,
    ms,
    xk,
    xr,
    xak,
    xar,
    xmat,
    xtail,
    tails,
    gb,
    ga,
    gh,
    gn,
    full,
    wmat,
    uk,
    ur,
    slot_ref,
    load_sem,
    rot_send,
    rot_recv,
    back_send,
    back_recv,
    mom_send,
    mom_recv,
    x_send,
    x_recv,
    own_send,
    own_recv,
    own_local,
    red_send,
    red_recv,
    out_send,
    out_recv,
):
    w = lax.axis_index("wide")
    n = lax.axis_index("narrow")
    x, z = w // 4, w % 4
    y, c = n // 2, n % 2
    is_even = w % 2 == 0
    is_odd = w % 2 == 1

    def wide_peer(offset):
        return ((x + offset[0]) % 4) * 4 + (z + offset[1]) % 4

    def narrow_peer(offset):
        return ((y + offset[0]) % 4) * 2 + (c + offset[1]) % 2

    def remote(src, dst, send, recv, where):
        return pltpu.make_async_remote_copy(
            src_ref=src,
            dst_ref=dst,
            send_sem=send,
            recv_sem=recv,
            device_id=where,
            device_id_type=MESH,
        )

    next_wide = {"wide": wide_peer((0, 1))}
    next_narrow = {"narrow": narrow_peer((0, 1))}

    def arrived(ref, sem, where):
        remote(ref, ref, sem, sem, where).wait_recv()

    def sent(ref, sem, where):
        remote(ref, ref, sem, sem, where).wait_send()

    loads = [
        pltpu.make_async_copy(mom_hbm.at[s], momv.at[s], load_sem.at[s]) for s in range(MOST)
    ]
    for load in loads:
        load.start()

    barrier = pltpu.get_barrier_semaphore()
    for offset in WIDE_OFFSETS:
        pl.semaphore_signal(
            barrier, inc=1, device_id={"wide": wide_peer(offset)}, device_id_type=MESH
        )
    for offset in NARROW_OFFSETS:
        pl.semaphore_signal(
            barrier, inc=1, device_id={"narrow": narrow_peer(offset)}, device_id_type=MESH
        )

    owners = [owner[k] for k in range(MATS)]
    slots = []
    for k in range(MATS):
        taken = jnp.int32(0)
        for before in range(k):
            taken = taken + jnp.where(owners[before] == owners[k], 1, 0)
        slots.append(taken)
        slot_ref[k] = taken

    tails[...] = jnp.zeros(tails.shape, F32)

    def pack_momentum(s):
        odd = jnp.int32(0)
        for k in range(1, MATS, 2):
            odd = odd + jnp.where((owners[k] == w) & (slots[k] == s), 1, 0)
        loads[s].wait()
        is_router = jnp.full((ROWS, COLS), odd, jnp.int32) == 1
        for j in range(WIDE):
            as_kv = momv[s, j * KVL : j * KVL + ROWS, :]
            as_router = momv[s, j * EXL : j * EXL + ROWS, :]
            msend[s, j, :, :COLS] = jnp.where(is_router, as_router, as_kv).astype(BF16)
            rest = momv[s, j * KVL + ROWS : (j + 1) * KVL, :]
            for t in range(TILES):
                tails[j, t * TAIL : (t + 1) * TAIL, :] = rest[:, t * BLK : (t + 1) * BLK]
        msend[s, :, :, COLS:] = tails[...].astype(BF16)

    def send_momentum(s):
        for offset in WIDE_OFFSETS:
            to = wide_peer(offset)
            remote(
                msend.at[s, to], marr.at[w, s], mom_send.at[0], mom_recv.at[0], {"wide": to}
            ).start()
        marr[w, s] = msend[s, w]

    pack_momentum(0)
    pl.semaphore_wait(barrier, len(WIDE_OFFSETS) + len(NARROW_OFFSETS))
    send_momentum(0)

    def gather_columns(part, source, target):
        for offset in NARROW_OFFSETS:
            to = narrow_peer(offset)
            remote(
                source.at[to], target.at[n], rot_send.at[part], rot_recv.at[part], {"narrow": to}
            ).start()
        target[n] = source[n]

    gather_columns(1, gr, rr)
    for t in range(TILES):
        cols = slice(t * BLK, (t + 1) * BLK)
        by_layer = jnp.swapaxes(gkv[:, :, cols].astype(F32), 0, 1)
        gp[:, :, cols] = by_layer[:, :ROWS].astype(BF16)
        tails[:LAYERS, t * TAIL : (t + 1) * TAIL, :] = by_layer[:, ROWS:]
    gp[:, :, COLS:] = tails[:LAYERS].astype(BF16)
    gather_columns(0, gp, rk)

    for s in range(1, MOST):
        pack_momentum(s)
        send_momentum(s)

    def rotate(source, target, count):
        def column(t, carry):
            cols = pl.ds(pl.multiple_of(t * BLK, BLK), BLK)
            blocks = [source[b, :, cols].astype(F32) for b in range(NARROW)]
            for bit in range(3):
                stride = 1 << bit
                mixed = list(blocks)
                for b in range(NARROW):
                    if not b & stride:
                        low, high = blocks[b], blocks[b + stride]
                        mixed[b] = ((low + high) * HALF_ROOT).astype(BF16)
                        mixed[b + stride] = ((low - high) * HALF_ROOT).astype(BF16)
                        if bit < 2:
                            mixed[b] = mixed[b].astype(F32)
                            mixed[b + stride] = mixed[b + stride].astype(F32)
                blocks = mixed
            for b in range(NARROW):
                target[b, :, cols] = blocks[b]
            return carry

        lax.fori_loop(0, count, column, 0)

    for part, source, turned, final in ((1, rr, tr, mr), (0, rk, tk, mk)):
        arrived(source.at[pl.ds(0, NARROW - 1)], rot_recv.at[part], next_narrow)
        rotate(source, turned, source.shape[2] // BLK)
        for offset in NARROW_OFFSETS:
            to = narrow_peer(offset)
            remote(
                turned.at[to], final.at[n], back_send.at[part], back_recv.at[part], {"narrow": to}
            ).start()
        final[n] = turned[n]
    for part, final in ((1, mr), (0, mk)):
        arrived(final.at[pl.ds(0, NARROW - 1)], back_recv.at[part], next_narrow)

    mats[...] = jnp.zeros(mats.shape, BF16)

    def by_matrix(layer, carry):
        mats[2 * layer] = mk[layer]
        mats[2 * layer + 1, :EXL, :COLS] = mr[layer]
        return carry

    lax.fori_loop(0, LAYERS, by_matrix, 0)

    def stage(o, carry):
        for s in range(MOST):
            held = jnp.int32(0)
            for k in range(MATS):
                held = held + jnp.where((owner[k] == o) & (slot_ref[k] == s), k, 0)
            ms[s, o] = mats[held]
        return carry

    lax.fori_loop(0, WIDE, stage, 0)
    arrived(marr.at[pl.ds(0, WIDE - 1)], mom_recv.at[0], next_wide)

    def push(layer, carry):
        for part, (source, target) in enumerate(((mk, xk), (mr, xr))):
            k = 2 * layer + part
            held = marr[owner[k], jnp.minimum(slot_ref[k], MOST - 1)]
            if part:
                held = held[:EXL, :COLS]
            fresh = source[layer].astype(F32)
            state = MOMENTUM_DECAY * held.astype(F32) + fresh
            target[layer] = (fresh + MOMENTUM_DECAY * state).astype(BF16)
        return carry

    lax.fori_loop(0, LAYERS, push, 0)

    for offset in WIDE_OFFSETS:
        to = wide_peer(offset)

        @pl.when(to % 2 == 0)
        def _():
            remote(
                xk.at[to // 2], xak.at[w], x_send.at[0], x_recv.at[0], {"wide": to}
            ).start()

        @pl.when(to % 2 == 1)
        def _():
            remote(
                xr.at[to // 2], xar.at[w], x_send.at[1], x_recv.at[0], {"wide": to}
            ).start()

    xmat[...] = jnp.zeros(xmat.shape, BF16)
    xtail[...] = jnp.zeros(xtail.shape, F32)

    @pl.when(is_even)
    def _():
        xak[w] = xk[w // 2]
        arrived(xak.at[pl.ds(0, WIDE - 1)], x_recv.at[0], next_wide)

    @pl.when(is_odd)
    def _():
        xar[w] = xr[w // 2]
        arrived(xar.at[pl.ds(0, WIDE - 1)], x_recv.at[0], next_wide)

    for s in range(MOST):
        for offset in WIDE_OFFSETS:
            to = wide_peer(offset)
            remote(
                ms.at[s, to], ma.at[s, w], own_send.at[0], own_recv.at[0], {"wide": to}
            ).start()
    stays = pltpu.make_async_copy(ms.at[:, w], ma.at[:, w], own_local.at[0])
    stays.start()

    @pl.when(is_even)
    def _():
        for j in range(WIDE):
            xmat[j * ROWS : (j + 1) * ROWS, :] = xak[j, :, :COLS]
            rest = xak[j, :, COLS:].astype(F32)
            for t in range(TILES):
                xtail[j * TAIL : (j + 1) * TAIL, t * BLK : (t + 1) * BLK] = rest[
                    t * TAIL : (t + 1) * TAIL
                ]
        xmat[WIDE * ROWS :, :] = xtail[...].astype(BF16)

    @pl.when(is_odd)
    def _():
        for j in range(WIDE):
            xmat[j * ROWS : j * ROWS + EXL, :] = xar[j]

    gram = lax.dot_general(
        xmat[...], xmat[...], (((1,), (1,)), ((), ())), preferred_element_type=F32
    )
    for b, (i, j) in enumerate(UPPER):
        gb[b] = gram[i * BLK : (i + 1) * BLK, j * BLK : (j + 1) * BLK]
    gb[15] = jnp.zeros((BLK, BLK), F32)

    partner = {"narrow": y * 2 + 1 - c}
    red = []

    def reduce_copy(src, dst, where):
        index = len(red)
        copy = remote(src, dst, red_send.at[index], red_recv.at[index], where)
        copy.start()
        red.append(copy)
        return copy

    pairs = [
        reduce_copy(gb.at[pl.ds(i * 8 + (1 - c) * 4, 4)], ga.at[i], partner) for i in range(2)
    ]
    around = [((y + step) % 4, (y + 4 - step) % 4) for step in (2, 1, 3)]
    scatter = []
    for i in range(2):
        pairs[i].wait_recv()
        gh[i] = gb[pl.ds(i * 8 + c * 4, 4)] + ga[i]
        scatter.append(
            [
                reduce_copy(gh.at[i, to], gn.at[i, step], {"narrow": to * 2 + c})
                for step, (to, _) in enumerate(around)
            ]
        )
    spread = []
    for i in range(2):
        for copy in scatter[i]:
            copy.wait_recv()
        mine = i * 8 + c * 4 + y
        full[mine] = gh[i, y] + gn[i, 0] + gn[i, 1] + gn[i, 2]
        spread.append(
            [
                reduce_copy(full.at[mine], full.at[mine], {"narrow": to * 2 + c})
                for to, _ in around
            ]
        )
        reduce_copy(full.at[mine], full.at[mine], partner)
    for i in range(2):
        for copy, (_, source) in zip(spread[i], around):
            copy.wait_recv()
            there = i * 8 + c * 4 + source
            reduce_copy(full.at[there], full.at[there], partner)
    for copy in red[11:12] + red[15:]:
        copy.wait_recv()

    blocks = {}
    trace = jnp.zeros((1, 1), F32)
    eye = (
        lax.broadcasted_iota(jnp.int32, (BLK, BLK), 0)
        == lax.broadcasted_iota(jnp.int32, (BLK, BLK), 1)
    )
    for b, (i, j) in enumerate(UPPER):
        block = full[b]
        blocks[i, j] = block
        if i == j:
            trace = trace + jnp.sum(jnp.where(eye, block, 0.0), keepdims=True)
        else:
            blocks[j, i] = block.T
    first = jnp.concatenate(
        [jnp.concatenate([blocks[i, j] for j in range(5)], axis=1) for i in range(5)], axis=0
    )[:KV, :KV]
    inverse_norm = 1.0 / (jnp.sqrt(trace) + EPSILON)
    current = inverse_norm * inverse_norm * first

    diagonal = (
        lax.broadcasted_iota(jnp.int32, (KV, KV), 0)
        == lax.broadcasted_iota(jnp.int32, (KV, KV), 1)
    )
    weight = None
    for turn in range(3):
        parts = split(current)
        square = product(parts, parts, 1 if turn == 2 else 3)
        cubic = split(POLY_CUBIC * current + POLY_QUINTIC * square)
        if turn == 0:
            weight = jnp.where(diagonal, POLY_LINEAR, 0.0) + (
                cubic[0].astype(F32) + cubic[1].astype(F32)
            )
        else:
            weight = POLY_LINEAR * weight + product(cubic, split(weight), 2 if turn == 2 else 3)
        if turn < 2:
            half_way = POLY_LINEAR * current + product(cubic, parts)
            current = POLY_LINEAR * half_way + product(cubic, split(half_way), 3 - turn)
    wmat[...] = jnp.concatenate(split(weight * (inverse_norm * GAIN)), axis=1)

    layer = w // 2

    def apply(rows):
        values = xmat[:KV]
        return jnp.dot(
            wmat[rows, :], jnp.concatenate([values, values], axis=0), preferred_element_type=F32
        )

    @pl.when(is_even)
    def _():
        last = apply(pl.ds(WIDE * ROWS, WIDE * TAIL))
        for j in range(WIDE):
            for t in range(TILES):
                tails[j, t * TAIL : (t + 1) * TAIL, :] = last[
                    j * TAIL : (j + 1) * TAIL, t * BLK : (t + 1) * BLK
                ]
        uk[:, :, COLS:] = tails[...].astype(BF16)

    def outgoing(step, carry):
        group = (x + 2 + step) % 4
        chunk = apply(pl.ds(pl.multiple_of(group * BLK, BLK), BLK)).astype(BF16)
        for i in range(4):
            to = group * 4 + i
            rows = chunk[i * ROWS : (i + 1) * ROWS]

            @pl.when(is_even)
            def _():
                uk[to, :, :COLS] = rows

            @pl.when(is_odd)
            def _():
                ur[to] = rows[:EXL]

            @pl.when(jnp.logical_and(is_even, to != w))
            def _():
                remote(
                    uk.at[to], out_kv.at[layer], out_send.at[0], out_recv.at[0], {"wide": to}
                ).start()

            @pl.when(jnp.logical_and(is_odd, to != w))
            def _():
                remote(
                    ur.at[to], out_r.at[layer], out_send.at[0], out_recv.at[1], {"wide": to}
                ).start()

        return carry

    lax.fori_loop(0, 4, outgoing, 0)

    @pl.when(is_even)
    def _():
        out_kv[layer] = uk[w]
        arrived(out_kv.at[pl.ds(0, 7)], out_recv.at[0], next_wide)
        arrived(out_r.at[pl.ds(0, 8)], out_recv.at[1], next_wide)
        sent(uk.at[pl.ds(0, 15)], out_send.at[0], next_wide)
        sent(xk.at[pl.ds(0, 7)], x_send.at[0], next_wide)
        sent(xr.at[pl.ds(0, 8)], x_send.at[1], next_wide)

    @pl.when(is_odd)
    def _():
        out_r[layer] = ur[w]
        arrived(out_kv.at[pl.ds(0, 8)], out_recv.at[0], next_wide)
        arrived(out_r.at[pl.ds(0, 7)], out_recv.at[1], next_wide)
        sent(ur.at[pl.ds(0, 15)], out_send.at[0], next_wide)
        sent(xk.at[pl.ds(0, 8)], x_send.at[0], next_wide)
        sent(xr.at[pl.ds(0, 7)], x_send.at[1], next_wide)

    arrived(ma.at[:, pl.ds(0, WIDE - 1)], own_recv.at[0], next_wide)
    stays.wait()
    sent(ms.at[:, pl.ds(0, WIDE - 1)], own_send.at[0], next_wide)
    sent(msend.at[:, pl.ds(0, WIDE - 1)], mom_send.at[0], next_wide)
    for part, source, turned in ((0, gp, tk), (1, gr, tr)):
        sent(source.at[pl.ds(0, NARROW - 1)], rot_send.at[part], next_narrow)
        sent(turned.at[pl.ds(0, NARROW - 1)], back_send.at[part], next_narrow)
    for copy in red:
        copy.wait_send()


def state_kernel(
    owner, mom, ma_hbm, out_kv, out_r, new_hbm, kv, router, ma, new, load_sem, store_sem
):
    w = lax.axis_index("wide")
    loads = [
        pltpu.make_async_copy(ma_hbm.at[s], ma.at[s], load_sem.at[s]) for s in range(MOST)
    ]
    for load in loads:
        load.start()
    stores = [
        pltpu.make_async_copy(new.at[s], new_hbm.at[s], store_sem.at[s]) for s in range(MOST)
    ]
    owners = [owner[k] for k in range(MATS)]
    kinds = [jnp.int32(0) for _ in range(MOST)]
    for k in range(MATS):
        slot = jnp.int32(0)
        for before in range(k):
            slot = slot + jnp.where(owners[before] == owners[k], 1, 0)
        for s in range(MOST):
            kinds[s] = kinds[s] + jnp.where((owners[k] == w) & (slot == s), 1 + k % 2, 0)

    def update_state(s, kind):
        @pl.when(kind == 1)
        def _():
            for j in range(WIDE):
                rows = slice(j * KVL, j * KVL + ROWS)
                new[s, rows, :] = MOMENTUM_DECAY * mom[s, rows, :] + ma[s, j, :, :COLS].astype(F32)
                rest = ma[s, j, :, COLS:].astype(F32)
                rows = slice(j * KVL + ROWS, (j + 1) * KVL)
                for t in range(TILES):
                    cols = slice(t * BLK, (t + 1) * BLK)
                    new[s, rows, cols] = (
                        MOMENTUM_DECAY * mom[s, rows, cols] + rest[t * TAIL : (t + 1) * TAIL]
                    )

        @pl.when(kind == 2)
        def _():
            for j in range(WIDE):
                rows = slice(j * EXL, (j + 1) * EXL)
                new[s, rows, :] = MOMENTUM_DECAY * mom[s, rows, :] + ma[
                    s, j, :EXL, :COLS
                ].astype(F32)
            new[s, EX:, :] = jnp.zeros((KV - EX, COLS), F32)

        @pl.when(kind == 0)
        def _():
            new[s] = jnp.zeros((KV, COLS), F32)

    for s in range(MOST):
        if s == 1:
            router[...] = out_r[...]
            for t in range(TILES):
                cols = slice(t * BLK, (t + 1) * BLK)
                by_row = jnp.swapaxes(out_kv[:, :, cols].astype(F32), 0, 1)
                kv[:ROWS, :, cols] = by_row.astype(BF16)
                rest = out_kv[:, :, COLS:].astype(F32)[:, t * TAIL : (t + 1) * TAIL]
                kv[ROWS:, :, cols] = jnp.swapaxes(rest, 0, 1).astype(BF16)
        loads[s].wait()
        update_state(s, kinds[s])
        stores[s].start()
    for store in stores:
        store.wait()


def local(grad_kv, grad_router, momentum, owner):
    vmem = pl.BlockSpec(memory_space=pltpu.VMEM)
    hbm = pl.BlockSpec(memory_space=pl.ANY)
    smem = pl.BlockSpec(memory_space=pltpu.SMEM)
    dma = pltpu.SemaphoreType.DMA
    kv_blocks = lambda *count: pltpu.VMEM(count + (ROWS, LANES), BF16)
    r_blocks = lambda count: pltpu.VMEM((count, EXL, COLS), BF16)
    square = lambda *count: pltpu.VMEM(count + (BLK, BLK), F32)
    update_kv, update_router, arrived = pl.pallas_call(
        step_kernel,
        out_shape=(
            jax.ShapeDtypeStruct((LAYERS, ROWS, LANES), BF16),
            jax.ShapeDtypeStruct((LAYERS, EXL, COLS), BF16),
            jax.ShapeDtypeStruct((MOST, WIDE, ROWS, LANES), BF16),
        ),
        in_specs=[vmem, vmem, hbm, smem],
        out_specs=(vmem, vmem, hbm),
        scratch_shapes=[
            pltpu.VMEM((MOST, KV, COLS), F32),
            kv_blocks(MOST, WIDE),
            kv_blocks(WIDE, MOST),
            kv_blocks(LAYERS),
            kv_blocks(NARROW),
            r_blocks(NARROW),
            kv_blocks(NARROW),
            r_blocks(NARROW),
            kv_blocks(LAYERS),
            r_blocks(LAYERS),
            kv_blocks(MATS),
            kv_blocks(MOST, WIDE),
            kv_blocks(LAYERS),
            r_blocks(LAYERS),
            kv_blocks(WIDE),
            r_blocks(WIDE),
            pltpu.VMEM((PADDED, COLS), BF16),
            pltpu.VMEM((PADDED - WIDE * ROWS, COLS), F32),
            pltpu.VMEM((WIDE, ROWS, BLK), F32),
            square(16),
            square(2, 4),
            square(2, 4),
            square(2, 3),
            square(16),
            pltpu.VMEM((KV, 2 * KV), BF16),
            kv_blocks(WIDE),
            r_blocks(WIDE),
            pltpu.SMEM((MATS,), jnp.int32),
            dma((MOST,)),
            dma((2,)),
            dma((2,)),
            dma((2,)),
            dma((2,)),
            dma((1,)),
            dma((1,)),
            dma((2,)),
            dma((1,)),
            dma((1,)),
            dma((1,)),
            dma((1,)),
            dma((22,)),
            dma((22,)),
            dma((1,)),
            dma((2,)),
        ],
        compiler_params=pltpu.CompilerParams(
            collective_id=0, has_side_effects=True, vmem_limit_bytes=50 * 2**20
        ),
        name="step",
    )(jnp.swapaxes(grad_kv, 0, 1), grad_router, momentum, owner)
    new_momentum, kv, router = pl.pallas_call(
        state_kernel,
        out_shape=(
            jax.ShapeDtypeStruct((MOST, KV, COLS), F32),
            jax.ShapeDtypeStruct((KVL, LAYERS, COLS), BF16),
            jax.ShapeDtypeStruct((LAYERS, EXL, COLS), BF16),
        ),
        in_specs=[smem, vmem, hbm, vmem, vmem],
        out_specs=(hbm, vmem, vmem),
        scratch_shapes=[
            kv_blocks(MOST, WIDE),
            pltpu.VMEM((MOST, KV, COLS), F32),
            dma((MOST,)),
            dma((MOST,)),
        ],
        compiler_params=pltpu.CompilerParams(vmem_limit_bytes=32 * 2**20),
        name="state",
    )(owner, momentum, arrived, update_kv, update_router)
    return jnp.swapaxes(kv, 0, 1), router, new_momentum


def solution(mesh):
    in_specs = (
        P(None, "wide", "narrow"),
        P(None, "wide", "narrow"),
        P("wide", None, "narrow"),
        P(),
    )
    out_specs = (P(None, "wide", "narrow"), P(None, "wide", "narrow"), P("wide", None, "narrow"))
    return jax.shard_map(local, mesh=mesh, in_specs=in_specs, out_specs=out_specs, check_vma=False)
```

```python
import math

import jax
import jax.numpy as jnp
from jax import lax
from jax.experimental import pallas as pl
from jax.experimental.pallas import tpu as pltpu
from jax.sharding import PartitionSpec as P

D = 7168
KV = 576
EX = 384
LAYERS = 8
MATS = 16
MOST = 3
WIDE = 16
NARROW = 8
COLS = D // NARROW
KVL = KV // WIDE
EXL = EX // WIDE
BLK = 128
PADDED = 640
ROWS = 32
LANES = COLS + BLK
TILES = COLS // BLK
TAIL = KVL - ROWS

MOMENTUM_DECAY = 0.95
POLY_LINEAR = 3.4445
POLY_CUBIC = -4.775
POLY_QUINTIC = 2.0315
EPSILON = 1e-07
HALF_ROOT = 0.7071067811865476
GAIN = 0.2 * math.sqrt(D)

MESH = pl.DeviceIdType.MESH
F32 = jnp.float32
BF16 = jnp.bfloat16


def hops(offset):
    return sum(min(step, 4 - step) for step in offset)


WIDE_OFFSETS = sorted(
    [(i, j) for i in range(4) for j in range(4) if i or j], key=lambda o: -hops(o)
)
NARROW_OFFSETS = [(2, 0), (2, 1), (1, 0), (3, 0), (1, 1), (3, 1), (0, 1)]
UPPER = [(i, j) for i in range(4) for j in range(i, 4)]
HALF = BLK // 2
PARTS = 3


def split(value):
    high = value.astype(BF16)
    low = (value - high.astype(F32)).astype(BF16)
    return high, low


def product(left, right, terms=3):
    lefts = [left[0], left[0], left[1]][:terms]
    rights = [right[0], right[1], right[0]][:terms]
    return jnp.dot(
        jnp.concatenate(lefts, axis=1),
        jnp.concatenate(rights, axis=0),
        preferred_element_type=F32,
    )


def step_kernel(
    gkv,
    gr,
    mom_hbm,
    owner,
    out_kv,
    out_r,
    ma,
    momv,
    msend,
    marr,
    gp,
    rk,
    rr,
    tk,
    tr,
    mk,
    mr,
    mats,
    ms,
    xk,
    xr,
    xak,
    xar,
    xmat,
    xtail,
    tails,
    gb,
    ga,
    gh,
    gn,
    full,
    wmat,
    uk,
    ur,
    slot_ref,
    load_sem,
    rot_send,
    rot_recv,
    back_send,
    back_recv,
    mom_send,
    mom_recv,
    x_send,
    x_recv,
    own_send,
    own_recv,
    own_local,
    red_send,
    red_recv,
    out_send,
    out_recv,
):
    w = lax.axis_index("wide")
    n = lax.axis_index("narrow")
    x, z = w // 4, w % 4
    y, c = n // 2, n % 2
    is_even = w % 2 == 0
    is_odd = w % 2 == 1

    def wide_peer(offset):
        return ((x + offset[0]) % 4) * 4 + (z + offset[1]) % 4

    def narrow_peer(offset):
        return ((y + offset[0]) % 4) * 2 + (c + offset[1]) % 2

    def remote(src, dst, send, recv, where):
        return pltpu.make_async_remote_copy(
            src_ref=src,
            dst_ref=dst,
            send_sem=send,
            recv_sem=recv,
            device_id=where,
            device_id_type=MESH,
        )

    next_wide = {"wide": wide_peer((0, 1))}
    next_narrow = {"narrow": narrow_peer((0, 1))}

    def arrived(ref, sem, where):
        remote(ref, ref, sem, sem, where).wait_recv()

    def sent(ref, sem, where):
        remote(ref, ref, sem, sem, where).wait_send()

    loads = [
        pltpu.make_async_copy(mom_hbm.at[s], momv.at[s], load_sem.at[s]) for s in range(MOST)
    ]
    for load in loads:
        load.start()

    barrier = pltpu.get_barrier_semaphore()
    for offset in WIDE_OFFSETS:
        pl.semaphore_signal(
            barrier, inc=1, device_id={"wide": wide_peer(offset)}, device_id_type=MESH
        )
    for offset in NARROW_OFFSETS:
        pl.semaphore_signal(
            barrier, inc=1, device_id={"narrow": narrow_peer(offset)}, device_id_type=MESH
        )

    owners = [owner[k] for k in range(MATS)]
    slots = []
    for k in range(MATS):
        taken = jnp.int32(0)
        for before in range(k):
            taken = taken + jnp.where(owners[before] == owners[k], 1, 0)
        slots.append(taken)
        slot_ref[k] = taken

    tails[...] = jnp.zeros(tails.shape, F32)

    def pack_momentum(s):
        odd = jnp.int32(0)
        for k in range(1, MATS, 2):
            odd = odd + jnp.where((owners[k] == w) & (slots[k] == s), 1, 0)
        loads[s].wait()
        is_router = jnp.full((ROWS, COLS), odd, jnp.int32) == 1
        for j in range(WIDE):
            as_kv = momv[s, j * KVL : j * KVL + ROWS, :]
            as_router = momv[s, j * EXL : j * EXL + ROWS, :]
            msend[s, j, :, :COLS] = jnp.where(is_router, as_router, as_kv).astype(BF16)
            rest = momv[s, j * KVL + ROWS : (j + 1) * KVL, :]
            for t in range(TILES):
                tails[j, t * TAIL : (t + 1) * TAIL, :] = rest[:, t * BLK : (t + 1) * BLK]
        msend[s, :, :, COLS:] = tails[...].astype(BF16)

    def send_momentum(s):
        for offset in WIDE_OFFSETS:
            to = wide_peer(offset)
            remote(
                msend.at[s, to], marr.at[w, s], mom_send.at[0], mom_recv.at[0], {"wide": to}
            ).start()
        marr[w, s] = msend[s, w]

    pack_momentum(0)
    pl.semaphore_wait(barrier, len(WIDE_OFFSETS) + len(NARROW_OFFSETS))
    send_momentum(0)

    def gather_columns(part, source, target):
        for offset in NARROW_OFFSETS:
            to = narrow_peer(offset)
            remote(
                source.at[to], target.at[n], rot_send.at[part], rot_recv.at[part], {"narrow": to}
            ).start()
        target[n] = source[n]

    gather_columns(1, gr, rr)
    for t in range(TILES):
        cols = slice(t * BLK, (t + 1) * BLK)
        by_layer = jnp.swapaxes(gkv[:, :, cols].astype(F32), 0, 1)
        gp[:, :, cols] = by_layer[:, :ROWS].astype(BF16)
        tails[:LAYERS, t * TAIL : (t + 1) * TAIL, :] = by_layer[:, ROWS:]
    gp[:, :, COLS:] = tails[:LAYERS].astype(BF16)
    gather_columns(0, gp, rk)

    for s in range(1, MOST):
        pack_momentum(s)
        send_momentum(s)

    def rotate(source, target, count):
        def column(t, carry):
            cols = pl.ds(pl.multiple_of(t * BLK, BLK), BLK)
            blocks = [source[b, :, cols].astype(F32) for b in range(NARROW)]
            for bit in range(3):
                stride = 1 << bit
                mixed = list(blocks)
                for b in range(NARROW):
                    if not b & stride:
                        low, high = blocks[b], blocks[b + stride]
                        mixed[b] = ((low + high) * HALF_ROOT).astype(BF16)
                        mixed[b + stride] = ((low - high) * HALF_ROOT).astype(BF16)
                        if bit < 2:
                            mixed[b] = mixed[b].astype(F32)
                            mixed[b + stride] = mixed[b + stride].astype(F32)
                blocks = mixed
            for b in range(NARROW):
                target[b, :, cols] = blocks[b]
            return carry

        lax.fori_loop(0, count, column, 0)

    for part, source, turned, final in ((1, rr, tr, mr), (0, rk, tk, mk)):
        arrived(source.at[pl.ds(0, NARROW - 1)], rot_recv.at[part], next_narrow)
        rotate(source, turned, source.shape[2] // BLK)
        for offset in NARROW_OFFSETS:
            to = narrow_peer(offset)
            remote(
                turned.at[to], final.at[n], back_send.at[part], back_recv.at[part], {"narrow": to}
            ).start()
        final[n] = turned[n]
    for part, final in ((1, mr), (0, mk)):
        arrived(final.at[pl.ds(0, NARROW - 1)], back_recv.at[part], next_narrow)

    mats[...] = jnp.zeros(mats.shape, BF16)

    def by_matrix(layer, carry):
        mats[2 * layer] = mk[layer]
        mats[2 * layer + 1, :EXL, :COLS] = mr[layer]
        return carry

    lax.fori_loop(0, LAYERS, by_matrix, 0)

    def stage(o, carry):
        for s in range(MOST):
            held = jnp.int32(0)
            for k in range(MATS):
                held = held + jnp.where((owner[k] == o) & (slot_ref[k] == s), k, 0)
            ms[s, o] = mats[held]
        return carry

    lax.fori_loop(0, WIDE, stage, 0)
    arrived(marr.at[pl.ds(0, WIDE - 1)], mom_recv.at[0], next_wide)

    def push(layer, carry):
        for part, (source, target) in enumerate(((mk, xk), (mr, xr))):
            k = 2 * layer + part
            held = marr[owner[k], jnp.minimum(slot_ref[k], MOST - 1)]
            if part:
                held = held[:EXL, :COLS]
            fresh = source[layer].astype(F32)
            state = MOMENTUM_DECAY * held.astype(F32) + fresh
            target[layer] = (fresh + MOMENTUM_DECAY * state).astype(BF16)
        return carry

    lax.fori_loop(0, LAYERS, push, 0)

    for offset in WIDE_OFFSETS:
        to = wide_peer(offset)

        @pl.when(to % 2 == 0)
        def _():
            remote(
                xk.at[to // 2], xak.at[w], x_send.at[0], x_recv.at[0], {"wide": to}
            ).start()

        @pl.when(to % 2 == 1)
        def _():
            remote(
                xr.at[to // 2], xar.at[w], x_send.at[1], x_recv.at[0], {"wide": to}
            ).start()

    xmat[...] = jnp.zeros(xmat.shape, BF16)
    xtail[...] = jnp.zeros(xtail.shape, F32)

    @pl.when(is_even)
    def _():
        xak[w] = xk[w // 2]
        sent(xk.at[pl.ds(0, 7)], x_send.at[0], next_wide)
        sent(xr.at[pl.ds(0, 8)], x_send.at[1], next_wide)

    @pl.when(is_odd)
    def _():
        xar[w] = xr[w // 2]
        sent(xk.at[pl.ds(0, 8)], x_send.at[0], next_wide)
        sent(xr.at[pl.ds(0, 7)], x_send.at[1], next_wide)

    for s in range(MOST):
        for offset in WIDE_OFFSETS[::-1]:
            to = wide_peer(offset)
            remote(
                ms.at[s, to], ma.at[s, w], own_send.at[0], own_recv.at[0], {"wide": to}
            ).start()
    stays = pltpu.make_async_copy(ms.at[:, w], ma.at[:, w], own_local.at[0])
    stays.start()

    @pl.when(is_even)
    def _():
        arrived(xak.at[pl.ds(0, WIDE - 1)], x_recv.at[0], next_wide)
        for j in range(WIDE):
            xmat[j * ROWS : (j + 1) * ROWS, :] = xak[j, :, :COLS]
            rest = xak[j, :, COLS:].astype(F32)
            for t in range(TILES):
                xtail[j * TAIL : (j + 1) * TAIL, t * BLK : (t + 1) * BLK] = rest[
                    t * TAIL : (t + 1) * TAIL
                ]
        xmat[WIDE * ROWS :, :] = xtail[...].astype(BF16)

    @pl.when(is_odd)
    def _():
        arrived(xar.at[pl.ds(0, WIDE - 1)], x_recv.at[0], next_wide)
        for j in range(WIDE):
            xmat[j * ROWS : j * ROWS + EXL, :] = xar[j]

    gram = lax.dot_general(
        xmat[...], xmat[...], (((1,), (1,)), ((), ())), preferred_element_type=F32
    )
    for b, (i, j) in enumerate(UPPER):
        for side in range(2):
            top = i * BLK + side * HALF
            gb[2 * b + side] = gram[top : top + HALF, j * BLK : (j + 1) * BLK]
    for j in range(4):
        gb[20 + j] = gram[4 * BLK : 4 * BLK + HALF, j * BLK : (j + 1) * BLK]
    corner = gram[4 * BLK : 4 * BLK + HALF, 4 * BLK :]
    left = lax.broadcasted_iota(jnp.int32, (HALF, BLK), 1) < HALF
    gb[1] = jnp.where(left, corner, gb[1])

    partner = {"narrow": y * 2 + 1 - c}
    red = []

    def reduce_copy(src, dst, where):
        index = len(red)
        copy = remote(src, dst, red_send.at[index], red_recv.at[index], where)
        copy.start()
        red.append(copy)
        return copy

    pairs = [
        reduce_copy(gb.at[pl.ds(i * 8 + (1 - c) * 4, 4)], ga.at[i], partner) for i in range(PARTS)
    ]
    around = [((y + step) % 4, (y + 4 - step) % 4) for step in (2, 1, 3)]
    scatter = []
    for i in range(PARTS):
        pairs[i].wait_recv()
        gh[i] = gb[pl.ds(i * 8 + c * 4, 4)] + ga[i]
        scatter.append(
            [
                reduce_copy(gh.at[i, to], gn.at[i, step], {"narrow": to * 2 + c})
                for step, (to, _) in enumerate(around)
            ]
        )
    spread = []
    back_to_core = []
    for i in range(PARTS):
        for copy in scatter[i]:
            copy.wait_recv()
        mine = i * 8 + c * 4 + y
        full[mine] = gh[i, y] + gn[i, 0] + gn[i, 1] + gn[i, 2]
        spread.append(
            [
                reduce_copy(full.at[mine], full.at[mine], {"narrow": to * 2 + c})
                for to, _ in around
            ]
        )
        back_to_core.append(reduce_copy(full.at[mine], full.at[mine], partner))
    for i in range(PARTS):
        for copy, (_, source) in zip(spread[i], around):
            copy.wait_recv()
            there = i * 8 + c * 4 + source
            back_to_core.append(reduce_copy(full.at[there], full.at[there], partner))
    for copy in back_to_core:
        copy.wait_recv()

    blocks = {}
    trace = jnp.zeros((1, 1), F32)
    eye = (
        lax.broadcasted_iota(jnp.int32, (BLK, BLK), 0)
        == lax.broadcasted_iota(jnp.int32, (BLK, BLK), 1)
    )
    for b, (i, j) in enumerate(UPPER):
        block = jnp.concatenate([full[2 * b], full[2 * b + 1]], axis=0)
        if b == 0:
            lower = lax.broadcasted_iota(jnp.int32, (BLK, BLK), 0) >= HALF
            early = lax.broadcasted_iota(jnp.int32, (BLK, BLK), 1) < HALF
            block = jnp.where(lower & early, block.T, block)
        blocks[i, j] = block
        if i == j:
            trace = trace + jnp.sum(jnp.where(eye, block, 0.0), keepdims=True)
        else:
            blocks[j, i] = block.T
    nothing = jnp.zeros((HALF, BLK), F32)
    for j in range(4):
        blocks[4, j] = jnp.concatenate([full[20 + j], nothing], axis=0)
        blocks[j, 4] = blocks[4, j].T
    corner = jnp.concatenate([jnp.where(left, full[1], 0.0), nothing], axis=0)
    blocks[4, 4] = corner
    trace = trace + jnp.sum(jnp.where(eye, corner, 0.0), keepdims=True)
    first = jnp.concatenate(
        [jnp.concatenate([blocks[i, j] for j in range(5)], axis=1) for i in range(5)], axis=0
    )[:KV, :KV]
    inverse_norm = 1.0 / (jnp.sqrt(trace) + EPSILON)
    current = inverse_norm * inverse_norm * first

    diagonal = (
        lax.broadcasted_iota(jnp.int32, (KV, KV), 0)
        == lax.broadcasted_iota(jnp.int32, (KV, KV), 1)
    )
    weight = None
    for turn in range(3):
        parts = split(current)
        square = product(parts, parts, 1 if turn == 2 else 3)
        cubic = split(POLY_CUBIC * current + POLY_QUINTIC * square)
        if turn == 0:
            weight = jnp.where(diagonal, POLY_LINEAR, 0.0) + (
                cubic[0].astype(F32) + cubic[1].astype(F32)
            )
        else:
            weight = POLY_LINEAR * weight + product(cubic, split(weight), 2 if turn == 2 else 3)
        if turn < 2:
            half_way = POLY_LINEAR * current + product(cubic, parts)
            current = POLY_LINEAR * half_way + product(cubic, split(half_way), 3 - turn)
    wmat[...] = jnp.concatenate(split(weight * (inverse_norm * GAIN)), axis=1)

    layer = w // 2

    def apply(rows):
        values = xmat[:KV]
        return jnp.dot(
            wmat[rows, :], jnp.concatenate([values, values], axis=0), preferred_element_type=F32
        )

    @pl.when(is_even)
    def _():
        last = apply(pl.ds(WIDE * ROWS, WIDE * TAIL))
        for j in range(WIDE):
            for t in range(TILES):
                tails[j, t * TAIL : (t + 1) * TAIL, :] = last[
                    j * TAIL : (j + 1) * TAIL, t * BLK : (t + 1) * BLK
                ]
        uk[:, :, COLS:] = tails[...].astype(BF16)

    def outgoing(step, carry):
        group = (x + 2 + step) % 4
        chunk = apply(pl.ds(pl.multiple_of(group * BLK, BLK), BLK)).astype(BF16)
        for i in range(4):
            to = group * 4 + i
            rows = chunk[i * ROWS : (i + 1) * ROWS]

            @pl.when(is_even)
            def _():
                uk[to, :, :COLS] = rows

            @pl.when(is_odd)
            def _():
                ur[to] = rows[:EXL]

            @pl.when(jnp.logical_and(is_even, to != w))
            def _():
                remote(
                    uk.at[to], out_kv.at[layer], out_send.at[0], out_recv.at[0], {"wide": to}
                ).start()

            @pl.when(jnp.logical_and(is_odd, to != w))
            def _():
                remote(
                    ur.at[to], out_r.at[layer], out_send.at[0], out_recv.at[1], {"wide": to}
                ).start()

        return carry

    lax.fori_loop(0, 4, outgoing, 0)

    @pl.when(is_even)
    def _():
        out_kv[layer] = uk[w]
        arrived(out_kv.at[pl.ds(0, 7)], out_recv.at[0], next_wide)
        arrived(out_r.at[pl.ds(0, 8)], out_recv.at[1], next_wide)
        sent(uk.at[pl.ds(0, 15)], out_send.at[0], next_wide)

    @pl.when(is_odd)
    def _():
        out_r[layer] = ur[w]
        arrived(out_kv.at[pl.ds(0, 8)], out_recv.at[0], next_wide)
        arrived(out_r.at[pl.ds(0, 7)], out_recv.at[1], next_wide)
        sent(ur.at[pl.ds(0, 15)], out_send.at[0], next_wide)

    arrived(ma.at[:, pl.ds(0, WIDE - 1)], own_recv.at[0], next_wide)
    stays.wait()
    sent(ms.at[:, pl.ds(0, WIDE - 1)], own_send.at[0], next_wide)
    sent(msend.at[:, pl.ds(0, WIDE - 1)], mom_send.at[0], next_wide)
    for part, source, turned in ((0, gp, tk), (1, gr, tr)):
        sent(source.at[pl.ds(0, NARROW - 1)], rot_send.at[part], next_narrow)
        sent(turned.at[pl.ds(0, NARROW - 1)], back_send.at[part], next_narrow)
    for copy in red:
        copy.wait_send()


def state_kernel(
    owner, mom, ma_hbm, out_kv, out_r, new_hbm, kv, router, ma, new, load_sem, store_sem
):
    w = lax.axis_index("wide")
    loads = [
        pltpu.make_async_copy(ma_hbm.at[s], ma.at[s], load_sem.at[s]) for s in range(MOST)
    ]
    for load in loads:
        load.start()
    stores = [
        pltpu.make_async_copy(new.at[s], new_hbm.at[s], store_sem.at[s]) for s in range(MOST)
    ]
    owners = [owner[k] for k in range(MATS)]
    kinds = [jnp.int32(0) for _ in range(MOST)]
    for k in range(MATS):
        slot = jnp.int32(0)
        for before in range(k):
            slot = slot + jnp.where(owners[before] == owners[k], 1, 0)
        for s in range(MOST):
            kinds[s] = kinds[s] + jnp.where((owners[k] == w) & (slot == s), 1 + k % 2, 0)

    def update_state(s, kind):
        @pl.when(kind == 1)
        def _():
            for j in range(WIDE):
                rows = slice(j * KVL, j * KVL + ROWS)
                new[s, rows, :] = MOMENTUM_DECAY * mom[s, rows, :] + ma[s, j, :, :COLS].astype(F32)
                rest = ma[s, j, :, COLS:].astype(F32)
                rows = slice(j * KVL + ROWS, (j + 1) * KVL)
                for t in range(TILES):
                    cols = slice(t * BLK, (t + 1) * BLK)
                    new[s, rows, cols] = (
                        MOMENTUM_DECAY * mom[s, rows, cols] + rest[t * TAIL : (t + 1) * TAIL]
                    )

        @pl.when(kind == 2)
        def _():
            for j in range(WIDE):
                rows = slice(j * EXL, (j + 1) * EXL)
                new[s, rows, :] = MOMENTUM_DECAY * mom[s, rows, :] + ma[
                    s, j, :EXL, :COLS
                ].astype(F32)
            new[s, EX:, :] = jnp.zeros((KV - EX, COLS), F32)

        @pl.when(kind == 0)
        def _():
            new[s] = jnp.zeros((KV, COLS), F32)

    for s in range(MOST):
        if s == 1:
            router[...] = out_r[...]
            for t in range(TILES):
                cols = slice(t * BLK, (t + 1) * BLK)
                by_row = jnp.swapaxes(out_kv[:, :, cols].astype(F32), 0, 1)
                kv[:ROWS, :, cols] = by_row.astype(BF16)
                rest = out_kv[:, :, COLS:].astype(F32)[:, t * TAIL : (t + 1) * TAIL]
                kv[ROWS:, :, cols] = jnp.swapaxes(rest, 0, 1).astype(BF16)
        loads[s].wait()
        update_state(s, kinds[s])
        stores[s].start()
    for store in stores:
        store.wait()


def local(grad_kv, grad_router, momentum, owner):
    vmem = pl.BlockSpec(memory_space=pltpu.VMEM)
    hbm = pl.BlockSpec(memory_space=pl.ANY)
    smem = pl.BlockSpec(memory_space=pltpu.SMEM)
    dma = pltpu.SemaphoreType.DMA
    kv_blocks = lambda *count: pltpu.VMEM(count + (ROWS, LANES), BF16)
    r_blocks = lambda count: pltpu.VMEM((count, EXL, COLS), BF16)
    pieces = lambda *count: pltpu.VMEM(count + (HALF, BLK), F32)
    update_kv, update_router, arrived = pl.pallas_call(
        step_kernel,
        out_shape=(
            jax.ShapeDtypeStruct((LAYERS, ROWS, LANES), BF16),
            jax.ShapeDtypeStruct((LAYERS, EXL, COLS), BF16),
            jax.ShapeDtypeStruct((MOST, WIDE, ROWS, LANES), BF16),
        ),
        in_specs=[vmem, vmem, hbm, smem],
        out_specs=(vmem, vmem, hbm),
        scratch_shapes=[
            pltpu.VMEM((MOST, KV, COLS), F32),
            kv_blocks(MOST, WIDE),
            kv_blocks(WIDE, MOST),
            kv_blocks(LAYERS),
            kv_blocks(NARROW),
            r_blocks(NARROW),
            kv_blocks(NARROW),
            r_blocks(NARROW),
            kv_blocks(LAYERS),
            r_blocks(LAYERS),
            kv_blocks(MATS),
            kv_blocks(MOST, WIDE),
            kv_blocks(LAYERS),
            r_blocks(LAYERS),
            kv_blocks(WIDE),
            r_blocks(WIDE),
            pltpu.VMEM((PADDED, COLS), BF16),
            pltpu.VMEM((PADDED - WIDE * ROWS, COLS), F32),
            pltpu.VMEM((WIDE, ROWS, BLK), F32),
            pieces(24),
            pieces(PARTS, 4),
            pieces(PARTS, 4),
            pieces(PARTS, 3),
            pieces(24),
            pltpu.VMEM((KV, 2 * KV), BF16),
            kv_blocks(WIDE),
            r_blocks(WIDE),
            pltpu.SMEM((MATS,), jnp.int32),
            dma((MOST,)),
            dma((2,)),
            dma((2,)),
            dma((2,)),
            dma((2,)),
            dma((1,)),
            dma((1,)),
            dma((2,)),
            dma((1,)),
            dma((1,)),
            dma((1,)),
            dma((1,)),
            dma((11 * PARTS,)),
            dma((11 * PARTS,)),
            dma((1,)),
            dma((2,)),
        ],
        compiler_params=pltpu.CompilerParams(
            collective_id=0, has_side_effects=True, vmem_limit_bytes=50 * 2**20
        ),
        name="step",
    )(jnp.swapaxes(grad_kv, 0, 1), grad_router, momentum, owner)
    new_momentum, kv, router = pl.pallas_call(
        state_kernel,
        out_shape=(
            jax.ShapeDtypeStruct((MOST, KV, COLS), F32),
            jax.ShapeDtypeStruct((KVL, LAYERS, COLS), BF16),
            jax.ShapeDtypeStruct((LAYERS, EXL, COLS), BF16),
        ),
        in_specs=[smem, vmem, hbm, vmem, vmem],
        out_specs=(hbm, vmem, vmem),
        scratch_shapes=[
            kv_blocks(MOST, WIDE),
            pltpu.VMEM((MOST, KV, COLS), F32),
            dma((MOST,)),
            dma((MOST,)),
        ],
        compiler_params=pltpu.CompilerParams(vmem_limit_bytes=32 * 2**20),
        name="state",
    )(owner, momentum, arrived, update_kv, update_router)
    return jnp.swapaxes(kv, 0, 1), router, new_momentum


def solution(mesh):
    in_specs = (
        P(None, "wide", "narrow"),
        P(None, "wide", "narrow"),
        P("wide", None, "narrow"),
        P(),
    )
    out_specs = (P(None, "wide", "narrow"), P(None, "wide", "narrow"), P("wide", None, "narrow"))
    return jax.shard_map(local, mesh=mesh, in_specs=in_specs, out_specs=out_specs, check_vma=False)
```

```python
import math

import jax
import jax.numpy as jnp
from jax import lax
from jax.experimental import pallas as pl
from jax.experimental.pallas import tpu as pltpu
from jax.sharding import PartitionSpec as P

D = 7168
KV = 576
EX = 384
LAYERS = 8
MATS = 16
MOST = 3
WIDE = 16
NARROW = 8
COLS = D // NARROW
KVL = KV // WIDE
EXL = EX // WIDE
BLK = 128
PADDED = 640
ROWS = 32
LANES = COLS + BLK
TILES = COLS // BLK
TAIL = KVL - ROWS

MOMENTUM_DECAY = 0.95
POLY_LINEAR = 3.4445
POLY_CUBIC = -4.775
POLY_QUINTIC = 2.0315
EPSILON = 1e-07
HALF_ROOT = 0.7071067811865476
GAIN = 0.2 * math.sqrt(D)

MESH = pl.DeviceIdType.MESH
F32 = jnp.float32
BF16 = jnp.bfloat16


def hops(offset):
    return sum(min(step, 4 - step) for step in offset)


WIDE_OFFSETS = sorted(
    [(i, j) for i in range(4) for j in range(4) if i or j], key=lambda o: -hops(o)
)
NARROW_OFFSETS = [(2, 0), (2, 1), (1, 0), (3, 0), (1, 1), (3, 1), (0, 1)]
UPPER = [(i, j) for i in range(4) for j in range(i, 4)]
HALF = BLK // 2
PARTS = 3


def split(value):
    high = value.astype(BF16)
    low = (value - high.astype(F32)).astype(BF16)
    return high, low


def product(left, right, terms=3):
    lefts = [left[0], left[0], left[1]][:terms]
    rights = [right[0], right[1], right[0]][:terms]
    return jnp.dot(
        jnp.concatenate(lefts, axis=1),
        jnp.concatenate(rights, axis=0),
        preferred_element_type=F32,
    )


def step_kernel(
    gkv,
    gr,
    mom_hbm,
    owner,
    out_kv,
    out_r,
    ma,
    momv,
    msend,
    marr,
    gp,
    rk,
    rr,
    tk,
    tr,
    mk,
    mr,
    mats,
    ms,
    xk,
    xr,
    xak,
    xar,
    xmat,
    xtail,
    tails,
    gb,
    ga,
    gh,
    gn,
    full,
    wmat,
    uk,
    ur,
    slot_ref,
    load_sem,
    rot_send,
    rot_recv,
    back_send,
    back_recv,
    mom_send,
    mom_recv,
    x_send,
    x_recv,
    own_send,
    own_recv,
    own_local,
    red_send,
    red_recv,
    out_send,
    out_recv,
):
    w = lax.axis_index("wide")
    n = lax.axis_index("narrow")
    x, z = w // 4, w % 4
    y, c = n // 2, n % 2
    is_even = w % 2 == 0
    is_odd = w % 2 == 1

    def wide_peer(offset):
        return ((x + offset[0]) % 4) * 4 + (z + offset[1]) % 4

    def narrow_peer(offset):
        return ((y + offset[0]) % 4) * 2 + (c + offset[1]) % 2

    def remote(src, dst, send, recv, where):
        return pltpu.make_async_remote_copy(
            src_ref=src,
            dst_ref=dst,
            send_sem=send,
            recv_sem=recv,
            device_id=where,
            device_id_type=MESH,
        )

    next_wide = {"wide": wide_peer((0, 1))}
    next_narrow = {"narrow": narrow_peer((0, 1))}

    def arrived(ref, sem, where):
        remote(ref, ref, sem, sem, where).wait_recv()

    def sent(ref, sem, where):
        remote(ref, ref, sem, sem, where).wait_send()

    loads = [
        pltpu.make_async_copy(mom_hbm.at[s], momv.at[s], load_sem.at[s]) for s in range(MOST)
    ]
    for load in loads:
        load.start()

    barrier = pltpu.get_barrier_semaphore()
    for offset in WIDE_OFFSETS:
        pl.semaphore_signal(
            barrier, inc=1, device_id={"wide": wide_peer(offset)}, device_id_type=MESH
        )
    for offset in NARROW_OFFSETS:
        pl.semaphore_signal(
            barrier, inc=1, device_id={"narrow": narrow_peer(offset)}, device_id_type=MESH
        )

    owners = [owner[k] for k in range(MATS)]
    slots = []
    for k in range(MATS):
        taken = jnp.int32(0)
        for before in range(k):
            taken = taken + jnp.where(owners[before] == owners[k], 1, 0)
        slots.append(taken)
        slot_ref[k] = taken

    tails[...] = jnp.zeros(tails.shape, F32)

    def pack_momentum(s):
        odd = jnp.int32(0)
        for k in range(1, MATS, 2):
            odd = odd + jnp.where((owners[k] == w) & (slots[k] == s), 1, 0)
        loads[s].wait()
        is_router = jnp.full((ROWS, COLS), odd, jnp.int32) == 1
        for j in range(WIDE):
            as_kv = momv[s, j * KVL : j * KVL + ROWS, :]
            as_router = momv[s, j * EXL : j * EXL + ROWS, :]
            msend[s, j, :, :COLS] = jnp.where(is_router, as_router, as_kv).astype(BF16)
            rest = momv[s, j * KVL + ROWS : (j + 1) * KVL, :]
            for t in range(TILES):
                tails[j, t * TAIL : (t + 1) * TAIL, :] = rest[:, t * BLK : (t + 1) * BLK]
        msend[s, :, :, COLS:] = tails[...].astype(BF16)

    def send_momentum(s):
        for offset in WIDE_OFFSETS[::-1]:
            to = wide_peer(offset)
            remote(
                msend.at[s, to], marr.at[w, s], mom_send.at[0], mom_recv.at[0], {"wide": to}
            ).start()
        marr[w, s] = msend[s, w]

    pack_momentum(0)
    pl.semaphore_wait(barrier, len(WIDE_OFFSETS) + len(NARROW_OFFSETS))
    send_momentum(0)

    def gather_columns(part, source, target):
        for offset in NARROW_OFFSETS:
            to = narrow_peer(offset)
            remote(
                source.at[to], target.at[n], rot_send.at[part], rot_recv.at[part], {"narrow": to}
            ).start()
        target[n] = source[n]

    gather_columns(1, gr, rr)
    for t in range(TILES):
        cols = slice(t * BLK, (t + 1) * BLK)
        by_layer = jnp.swapaxes(gkv[:, :, cols].astype(F32), 0, 1)
        gp[:, :, cols] = by_layer[:, :ROWS].astype(BF16)
        tails[:LAYERS, t * TAIL : (t + 1) * TAIL, :] = by_layer[:, ROWS:]
    gp[:, :, COLS:] = tails[:LAYERS].astype(BF16)
    gather_columns(0, gp, rk)

    for s in range(1, MOST):
        pack_momentum(s)
        send_momentum(s)

    def rotate(source, target, count):
        def column(t, carry):
            cols = pl.ds(pl.multiple_of(t * BLK, BLK), BLK)
            blocks = [source[b, :, cols].astype(F32) for b in range(NARROW)]
            for bit in range(3):
                stride = 1 << bit
                mixed = list(blocks)
                for b in range(NARROW):
                    if not b & stride:
                        low, high = blocks[b], blocks[b + stride]
                        mixed[b] = ((low + high) * HALF_ROOT).astype(BF16)
                        mixed[b + stride] = ((low - high) * HALF_ROOT).astype(BF16)
                        if bit < 2:
                            mixed[b] = mixed[b].astype(F32)
                            mixed[b + stride] = mixed[b + stride].astype(F32)
                blocks = mixed
            for b in range(NARROW):
                target[b, :, cols] = blocks[b]
            return carry

        lax.fori_loop(0, count, column, 0)

    for part, source, turned, final in ((1, rr, tr, mr), (0, rk, tk, mk)):
        arrived(source.at[pl.ds(0, NARROW - 1)], rot_recv.at[part], next_narrow)
        rotate(source, turned, source.shape[2] // BLK)
        for offset in NARROW_OFFSETS:
            to = narrow_peer(offset)
            remote(
                turned.at[to], final.at[n], back_send.at[part], back_recv.at[part], {"narrow": to}
            ).start()
        final[n] = turned[n]
    for part, final in ((1, mr), (0, mk)):
        arrived(final.at[pl.ds(0, NARROW - 1)], back_recv.at[part], next_narrow)

    mats[...] = jnp.zeros(mats.shape, BF16)

    def by_matrix(layer, carry):
        mats[2 * layer] = mk[layer]
        mats[2 * layer + 1, :EXL, :COLS] = mr[layer]
        return carry

    lax.fori_loop(0, LAYERS, by_matrix, 0)

    def stage(o, carry):
        for s in range(MOST):
            held = jnp.int32(0)
            for k in range(MATS):
                held = held + jnp.where((owner[k] == o) & (slot_ref[k] == s), k, 0)
            ms[s, o] = mats[held]
        return carry

    lax.fori_loop(0, WIDE, stage, 0)
    arrived(marr.at[pl.ds(0, WIDE - 1)], mom_recv.at[0], next_wide)

    def push(step, carry):
        layer = (w // 2 + 1 + step) % LAYERS
        for part, (source, target, landing) in enumerate(((mk, xk, xak), (mr, xr, xar))):
            k = 2 * layer + part
            held = marr[owner[k], jnp.minimum(slot_ref[k], MOST - 1)]
            if part:
                held = held[:EXL, :COLS]
            fresh = source[layer].astype(F32)
            state = MOMENTUM_DECAY * held.astype(F32) + fresh
            target[layer] = (fresh + MOMENTUM_DECAY * state).astype(BF16)

            @pl.when(k != w)
            def _():
                remote(
                    target.at[layer], landing.at[w], x_send.at[part], x_recv.at[0], {"wide": k}
                ).start()

        return carry

    lax.fori_loop(0, LAYERS, push, 0)

    xmat[...] = jnp.zeros(xmat.shape, BF16)
    xtail[...] = jnp.zeros(xtail.shape, F32)

    @pl.when(is_even)
    def _():
        xak[w] = xk[w // 2]
        sent(xk.at[pl.ds(0, 7)], x_send.at[0], next_wide)
        sent(xr.at[pl.ds(0, 8)], x_send.at[1], next_wide)

    @pl.when(is_odd)
    def _():
        xar[w] = xr[w // 2]
        sent(xk.at[pl.ds(0, 8)], x_send.at[0], next_wide)
        sent(xr.at[pl.ds(0, 7)], x_send.at[1], next_wide)

    for s in range(MOST):
        for offset in WIDE_OFFSETS[::-1]:
            to = wide_peer(offset)
            remote(
                ms.at[s, to], ma.at[s, w], own_send.at[0], own_recv.at[0], {"wide": to}
            ).start()
    stays = pltpu.make_async_copy(ms.at[:, w], ma.at[:, w], own_local.at[0])
    stays.start()

    @pl.when(is_even)
    def _():
        arrived(xak.at[pl.ds(0, WIDE - 1)], x_recv.at[0], next_wide)
        for j in range(WIDE):
            xmat[j * ROWS : (j + 1) * ROWS, :] = xak[j, :, :COLS]
            rest = xak[j, :, COLS:].astype(F32)
            for t in range(TILES):
                xtail[j * TAIL : (j + 1) * TAIL, t * BLK : (t + 1) * BLK] = rest[
                    t * TAIL : (t + 1) * TAIL
                ]
        xmat[WIDE * ROWS :, :] = xtail[...].astype(BF16)

    @pl.when(is_odd)
    def _():
        arrived(xar.at[pl.ds(0, WIDE - 1)], x_recv.at[0], next_wide)
        for j in range(WIDE):
            xmat[j * ROWS : j * ROWS + EXL, :] = xar[j]

    gram = lax.dot_general(
        xmat[...], xmat[...], (((1,), (1,)), ((), ())), preferred_element_type=F32
    )
    for b, (i, j) in enumerate(UPPER):
        for side in range(2):
            top = i * BLK + side * HALF
            gb[2 * b + side] = gram[top : top + HALF, j * BLK : (j + 1) * BLK]
    for j in range(4):
        gb[20 + j] = gram[4 * BLK : 4 * BLK + HALF, j * BLK : (j + 1) * BLK]
    corner = gram[4 * BLK : 4 * BLK + HALF, 4 * BLK :]
    left = lax.broadcasted_iota(jnp.int32, (HALF, BLK), 1) < HALF
    gb[1] = jnp.where(left, corner, gb[1])

    partner = {"narrow": y * 2 + 1 - c}
    red = []

    def reduce_copy(src, dst, where):
        index = len(red)
        copy = remote(src, dst, red_send.at[index], red_recv.at[index], where)
        copy.start()
        red.append(copy)
        return copy

    pairs = [
        reduce_copy(gb.at[pl.ds(i * 8 + (1 - c) * 4, 4)], ga.at[i], partner) for i in range(PARTS)
    ]
    around = [((y + step) % 4, (y + 4 - step) % 4) for step in (2, 1, 3)]
    scatter = []
    for i in range(PARTS):
        pairs[i].wait_recv()
        gh[i] = gb[pl.ds(i * 8 + c * 4, 4)] + ga[i]
        scatter.append(
            [
                reduce_copy(gh.at[i, to], gn.at[i, step], {"narrow": to * 2 + c})
                for step, (to, _) in enumerate(around)
            ]
        )
    spread = []
    back_to_core = []
    for i in range(PARTS):
        for copy in scatter[i]:
            copy.wait_recv()
        mine = i * 8 + c * 4 + y
        full[mine] = gh[i, y] + gn[i, 0] + gn[i, 1] + gn[i, 2]
        spread.append(
            [
                reduce_copy(full.at[mine], full.at[mine], {"narrow": to * 2 + c})
                for to, _ in around
            ]
        )
        back_to_core.append(reduce_copy(full.at[mine], full.at[mine], partner))
    for i in range(PARTS):
        for copy, (_, source) in zip(spread[i], around):
            copy.wait_recv()
            there = i * 8 + c * 4 + source
            back_to_core.append(reduce_copy(full.at[there], full.at[there], partner))
    for copy in back_to_core:
        copy.wait_recv()

    blocks = {}
    trace = jnp.zeros((1, 1), F32)
    eye = (
        lax.broadcasted_iota(jnp.int32, (BLK, BLK), 0)
        == lax.broadcasted_iota(jnp.int32, (BLK, BLK), 1)
    )
    for b, (i, j) in enumerate(UPPER):
        block = jnp.concatenate([full[2 * b], full[2 * b + 1]], axis=0)
        if b == 0:
            lower = lax.broadcasted_iota(jnp.int32, (BLK, BLK), 0) >= HALF
            early = lax.broadcasted_iota(jnp.int32, (BLK, BLK), 1) < HALF
            block = jnp.where(lower & early, block.T, block)
        blocks[i, j] = block
        if i == j:
            trace = trace + jnp.sum(jnp.where(eye, block, 0.0), keepdims=True)
        else:
            blocks[j, i] = block.T
    nothing = jnp.zeros((HALF, BLK), F32)
    for j in range(4):
        blocks[4, j] = jnp.concatenate([full[20 + j], nothing], axis=0)
        blocks[j, 4] = blocks[4, j].T
    corner = jnp.concatenate([jnp.where(left, full[1], 0.0), nothing], axis=0)
    blocks[4, 4] = corner
    trace = trace + jnp.sum(jnp.where(eye, corner, 0.0), keepdims=True)
    first = jnp.concatenate(
        [jnp.concatenate([blocks[i, j] for j in range(5)], axis=1) for i in range(5)], axis=0
    )[:KV, :KV]
    inverse_norm = 1.0 / (jnp.sqrt(trace) + EPSILON)
    current = inverse_norm * inverse_norm * first

    diagonal = (
        lax.broadcasted_iota(jnp.int32, (KV, KV), 0)
        == lax.broadcasted_iota(jnp.int32, (KV, KV), 1)
    )
    weight = None
    for turn in range(3):
        parts = split(current)
        square = product(parts, parts, 1 if turn == 2 else 3)
        cubic = split(POLY_CUBIC * current + POLY_QUINTIC * square)
        if turn == 0:
            weight = jnp.where(diagonal, POLY_LINEAR, 0.0) + (
                cubic[0].astype(F32) + cubic[1].astype(F32)
            )
        else:
            weight = POLY_LINEAR * weight + product(cubic, split(weight), 2 if turn == 2 else 3)
        if turn < 2:
            half_way = POLY_LINEAR * current + product(cubic, parts)
            current = POLY_LINEAR * half_way + product(cubic, split(half_way), 3 - turn)
    wmat[...] = jnp.concatenate(split(weight * (inverse_norm * GAIN)), axis=1)

    layer = w // 2

    def apply(rows):
        values = xmat[:KV]
        return jnp.dot(
            wmat[rows, :], jnp.concatenate([values, values], axis=0), preferred_element_type=F32
        )

    @pl.when(is_even)
    def _():
        last = apply(pl.ds(WIDE * ROWS, WIDE * TAIL))
        for j in range(WIDE):
            for t in range(TILES):
                tails[j, t * TAIL : (t + 1) * TAIL, :] = last[
                    j * TAIL : (j + 1) * TAIL, t * BLK : (t + 1) * BLK
                ]
        uk[:, :, COLS:] = tails[...].astype(BF16)

    def outgoing(step, carry):
        group = (x + 2 + step) % 4
        chunk = apply(pl.ds(pl.multiple_of(group * BLK, BLK), BLK)).astype(BF16)
        for i in range(4):
            to = group * 4 + i
            rows = chunk[i * ROWS : (i + 1) * ROWS]

            @pl.when(is_even)
            def _():
                uk[to, :, :COLS] = rows

            @pl.when(is_odd)
            def _():
                ur[to] = rows[:EXL]

            @pl.when(jnp.logical_and(is_even, to != w))
            def _():
                remote(
                    uk.at[to], out_kv.at[layer], out_send.at[0], out_recv.at[0], {"wide": to}
                ).start()

            @pl.when(jnp.logical_and(is_odd, to != w))
            def _():
                remote(
                    ur.at[to], out_r.at[layer], out_send.at[0], out_recv.at[1], {"wide": to}
                ).start()

        return carry

    lax.fori_loop(0, 4, outgoing, 0)

    @pl.when(is_even)
    def _():
        out_kv[layer] = uk[w]
        arrived(out_kv.at[pl.ds(0, 7)], out_recv.at[0], next_wide)
        arrived(out_r.at[pl.ds(0, 8)], out_recv.at[1], next_wide)
        sent(uk.at[pl.ds(0, 15)], out_send.at[0], next_wide)

    @pl.when(is_odd)
    def _():
        out_r[layer] = ur[w]
        arrived(out_kv.at[pl.ds(0, 8)], out_recv.at[0], next_wide)
        arrived(out_r.at[pl.ds(0, 7)], out_recv.at[1], next_wide)
        sent(ur.at[pl.ds(0, 15)], out_send.at[0], next_wide)

    arrived(ma.at[:, pl.ds(0, WIDE - 1)], own_recv.at[0], next_wide)
    stays.wait()
    sent(ms.at[:, pl.ds(0, WIDE - 1)], own_send.at[0], next_wide)
    sent(msend.at[:, pl.ds(0, WIDE - 1)], mom_send.at[0], next_wide)
    for part, source, turned in ((0, gp, tk), (1, gr, tr)):
        sent(source.at[pl.ds(0, NARROW - 1)], rot_send.at[part], next_narrow)
        sent(turned.at[pl.ds(0, NARROW - 1)], back_send.at[part], next_narrow)
    for copy in red:
        copy.wait_send()


def state_kernel(
    owner, mom, ma_hbm, out_kv, out_r, new_hbm, kv, router, ma, new, load_sem, store_sem
):
    w = lax.axis_index("wide")
    loads = [
        pltpu.make_async_copy(ma_hbm.at[s], ma.at[s], load_sem.at[s]) for s in range(MOST)
    ]
    for load in loads:
        load.start()
    stores = [
        pltpu.make_async_copy(new.at[s], new_hbm.at[s], store_sem.at[s]) for s in range(MOST)
    ]
    owners = [owner[k] for k in range(MATS)]
    kinds = [jnp.int32(0) for _ in range(MOST)]
    for k in range(MATS):
        slot = jnp.int32(0)
        for before in range(k):
            slot = slot + jnp.where(owners[before] == owners[k], 1, 0)
        for s in range(MOST):
            kinds[s] = kinds[s] + jnp.where((owners[k] == w) & (slot == s), 1 + k % 2, 0)

    def update_state(s, kind):
        @pl.when(kind == 1)
        def _():
            for j in range(WIDE):
                rows = slice(j * KVL, j * KVL + ROWS)
                new[s, rows, :] = MOMENTUM_DECAY * mom[s, rows, :] + ma[s, j, :, :COLS].astype(F32)
                rest = ma[s, j, :, COLS:].astype(F32)
                rows = slice(j * KVL + ROWS, (j + 1) * KVL)
                for t in range(TILES):
                    cols = slice(t * BLK, (t + 1) * BLK)
                    new[s, rows, cols] = (
                        MOMENTUM_DECAY * mom[s, rows, cols] + rest[t * TAIL : (t + 1) * TAIL]
                    )

        @pl.when(kind == 2)
        def _():
            for j in range(WIDE):
                rows = slice(j * EXL, (j + 1) * EXL)
                new[s, rows, :] = MOMENTUM_DECAY * mom[s, rows, :] + ma[
                    s, j, :EXL, :COLS
                ].astype(F32)
            new[s, EX:, :] = jnp.zeros((KV - EX, COLS), F32)

        @pl.when(kind == 0)
        def _():
            new[s] = jnp.zeros((KV, COLS), F32)

    for s in range(MOST):
        if s == 1:
            router[...] = out_r[...]
            for t in range(TILES):
                cols = slice(t * BLK, (t + 1) * BLK)
                by_row = jnp.swapaxes(out_kv[:, :, cols].astype(F32), 0, 1)
                kv[:ROWS, :, cols] = by_row.astype(BF16)
                rest = out_kv[:, :, COLS:].astype(F32)[:, t * TAIL : (t + 1) * TAIL]
                kv[ROWS:, :, cols] = jnp.swapaxes(rest, 0, 1).astype(BF16)
        loads[s].wait()
        update_state(s, kinds[s])
        stores[s].start()
    for store in stores:
        store.wait()


def local(grad_kv, grad_router, momentum, owner):
    vmem = pl.BlockSpec(memory_space=pltpu.VMEM)
    hbm = pl.BlockSpec(memory_space=pl.ANY)
    smem = pl.BlockSpec(memory_space=pltpu.SMEM)
    dma = pltpu.SemaphoreType.DMA
    kv_blocks = lambda *count: pltpu.VMEM(count + (ROWS, LANES), BF16)
    r_blocks = lambda count: pltpu.VMEM((count, EXL, COLS), BF16)
    pieces = lambda *count: pltpu.VMEM(count + (HALF, BLK), F32)
    update_kv, update_router, arrived = pl.pallas_call(
        step_kernel,
        out_shape=(
            jax.ShapeDtypeStruct((LAYERS, ROWS, LANES), BF16),
            jax.ShapeDtypeStruct((LAYERS, EXL, COLS), BF16),
            jax.ShapeDtypeStruct((MOST, WIDE, ROWS, LANES), BF16),
        ),
        in_specs=[vmem, vmem, hbm, smem],
        out_specs=(vmem, vmem, hbm),
        scratch_shapes=[
            pltpu.VMEM((MOST, KV, COLS), F32),
            kv_blocks(MOST, WIDE),
            kv_blocks(WIDE, MOST),
            kv_blocks(LAYERS),
            kv_blocks(NARROW),
            r_blocks(NARROW),
            kv_blocks(NARROW),
            r_blocks(NARROW),
            kv_blocks(LAYERS),
            r_blocks(LAYERS),
            kv_blocks(MATS),
            kv_blocks(MOST, WIDE),
            kv_blocks(LAYERS),
            r_blocks(LAYERS),
            kv_blocks(WIDE),
            r_blocks(WIDE),
            pltpu.VMEM((PADDED, COLS), BF16),
            pltpu.VMEM((PADDED - WIDE * ROWS, COLS), F32),
            pltpu.VMEM((WIDE, ROWS, BLK), F32),
            pieces(24),
            pieces(PARTS, 4),
            pieces(PARTS, 4),
            pieces(PARTS, 3),
            pieces(24),
            pltpu.VMEM((KV, 2 * KV), BF16),
            kv_blocks(WIDE),
            r_blocks(WIDE),
            pltpu.SMEM((MATS,), jnp.int32),
            dma((MOST,)),
            dma((2,)),
            dma((2,)),
            dma((2,)),
            dma((2,)),
            dma((1,)),
            dma((1,)),
            dma((2,)),
            dma((1,)),
            dma((1,)),
            dma((1,)),
            dma((1,)),
            dma((11 * PARTS,)),
            dma((11 * PARTS,)),
            dma((1,)),
            dma((2,)),
        ],
        compiler_params=pltpu.CompilerParams(
            collective_id=0, has_side_effects=True, vmem_limit_bytes=50 * 2**20
        ),
        name="step",
    )(jnp.swapaxes(grad_kv, 0, 1), grad_router, momentum, owner)
    new_momentum, kv, router = pl.pallas_call(
        state_kernel,
        out_shape=(
            jax.ShapeDtypeStruct((MOST, KV, COLS), F32),
            jax.ShapeDtypeStruct((KVL, LAYERS, COLS), BF16),
            jax.ShapeDtypeStruct((LAYERS, EXL, COLS), BF16),
        ),
        in_specs=[smem, vmem, hbm, vmem, vmem],
        out_specs=(hbm, vmem, vmem),
        scratch_shapes=[
            kv_blocks(MOST, WIDE),
            pltpu.VMEM((MOST, KV, COLS), F32),
            dma((MOST,)),
            dma((MOST,)),
        ],
        compiler_params=pltpu.CompilerParams(vmem_limit_bytes=32 * 2**20),
        name="state",
    )(owner, momentum, arrived, update_kv, update_router)
    return jnp.swapaxes(kv, 0, 1), router, new_momentum


def solution(mesh):
    in_specs = (
        P(None, "wide", "narrow"),
        P(None, "wide", "narrow"),
        P("wide", None, "narrow"),
        P(),
    )
    out_specs = (P(None, "wide", "narrow"), P(None, "wide", "narrow"), P("wide", None, "narrow"))
    return jax.shard_map(local, mesh=mesh, in_specs=in_specs, out_specs=out_specs, check_vma=False)
```
